32 devices in a mesh: fsdp: 4 (over z), ctx: 2 (over x), tp: 4 (over y, core).
Axes of the slice: x: 2, y: 2, z: 4, core: 2. Of those that a mesh axis runs over, the one named last changes fastest.
Arguments:
- hidden_in: bfloat16 [4, 4096, 768], P('fsdp', 'ctx'), may hold values from -6 to 6
- segments: int32 [4, 4096], P('fsdp', 'ctx'), may hold values from 0 to 7, as said below
- positions: int32 [4, 4096], P('fsdp', 'ctx'), may hold values from 0 to 8191, as said below
- norm_gains: bfloat16 [2, 768], P(None, 'fsdp'), may hold values from 0.099609375 to 1.8984375
- norm_biases: bfloat16 [2, 768], P(None, 'fsdp'), may hold values from -2 to 2
- qkv_weight: bfloat16 [3, 768, 768], P(None, 'fsdp', 'tp'), may hold values from -0.21875 to 0.21875
- qkv_bias: bfloat16 [3, 12, 64], P(None, 'tp', 'fsdp'), may hold values from -2 to 2
- out_weight: bfloat16 [768, 768], P('tp', 'fsdp'), may hold values from -0.625 to 0.625
- up_weight: bfloat16 [768, 3072], P('fsdp', 'tp'), may hold values from -0.21875 to 0.21875
- up_bias: bfloat16 [48, 64], P('tp', 'fsdp'), may hold values from -2 to 2
- down_weight: bfloat16 [3072, 768], P('tp', 'fsdp'), may hold values from -0.109375 to 0.109375
- branch_biases: bfloat16 [2, 768], P(None, 'fsdp'), may hold values from -2 to 2
- out_grad: bfloat16 [4, 4096, 768], P('fsdp', 'ctx'), may hold values from -6 to 6
Outputs:
- hidden_out: bfloat16 [4, 4096, 768], P('fsdp', 'ctx')
- input_grad: bfloat16 [4, 4096, 768], P('fsdp', 'ctx')
- norm_gains_grad: float32 [2, 768], P(None, 'fsdp')
- norm_biases_grad: float32 [2, 768], P(None, 'fsdp')
- qkv_weight_grad: float32 [3, 768, 768], P(None, 'fsdp', 'tp')
- qkv_bias_grad: float32 [3, 12, 64], P(None, 'tp', 'fsdp')
- out_weight_grad: float32 [768, 768], P('tp', 'fsdp')
- up_weight_grad: float32 [768, 3072], P('fsdp', 'tp')
- up_bias_grad: float32 [48, 64], P('tp', 'fsdp')
- down_weight_grad: float32 [3072, 768], P('tp', 'fsdp')
- branch_biases_grad: float32 [2, 768], P(None, 'fsdp')
The draws below stay inside these ranges and needn't reach their ends.
Inputs may be any that keep to these rules, and one draw needn't show every extreme that they name: `segments`: within a row segment numbers never fall and start at 0; every row holds 8 documents, and one of them covers the positions 1536 to 2560 of the row. Within a document positions rise by one from token to token; the last document of every row ends at 8191.
All inputs are finite; a program needn't handle non-finite values.
Results may differ from the reference program's by a relative error of at most 0.012.
Values may be sent and summed in bfloat16 or wider, within the bound.
A program may use at most 192 MiB of HBM per device.

```python
import jax
import jax.numpy as jnp
import numpy as np
from jax import lax

D = 768
HD = 64
FF = 3072
HEADS = 12
ROT = 16
NDOC = 8
SEQ = 4096
ROWS = 4


def doc_layout(key):
    middle = SEQ // 2
    margin = SEQ // 8
    candidates = np.array([spot for spot in range(1, SEQ) if spot < middle - margin or spot > middle + margin], dtype=np.int32)

    def one_row(row_key):
        pick_key, offset_key = jax.random.split(row_key)
        chosen = jax.random.permutation(pick_key, jnp.asarray(candidates))[:NDOC - 1]
        starts = jnp.sort(chosen)
        places = jnp.arange(SEQ, dtype=jnp.int32)
        segment = jnp.sum((places[:, None] >= starts[None, :]).astype(jnp.int32), axis=1).astype(jnp.int32)
        begins = jnp.concatenate([jnp.zeros((1,), jnp.int32), starts]).astype(jnp.int32)
        offsets = jax.random.randint(offset_key, (NDOC,), 0, SEQ + 1, dtype=jnp.int32)
        offsets = offsets.at[NDOC - 1].set(SEQ + starts[NDOC - 2])
        position = offsets[segment] + places - begins[segment]
        return (segment, position.astype(jnp.int32))
    return jax.vmap(one_row)(jax.random.split(key, ROWS))


def draw_segments(key, part):
    return doc_layout(key)[0]


def draw_positions(key, part):
    return doc_layout(key)[1]


def block_levels(own_key, dims, pieces, low, top_value):
    def one(dim, blocks):
        heights = jax.random.uniform(jax.random.fold_in(jax.random.fold_in(own_key, 6), dim), (blocks,), jnp.float32, low / len(pieces), top_value / len(pieces))
        return jnp.repeat(jnp.exp(heights), dims[dim] // blocks).reshape((-1,) + (1,) * (len(dims) - dim - 1))

    gain = one(*pieces[0])
    for cut in pieces[1:]:
        gain = gain * one(*cut)
    return gain


def noise(stream_key, extent, scale, reach, cuts=(), kind=jnp.bfloat16):
    entries = scale * jax.random.normal(stream_key, extent, jnp.float32)
    if cuts:
        entries = entries * block_levels(stream_key, extent, cuts, -0.22, 0.18)
    return jnp.clip(entries, -reach, reach).astype(kind)


def setup_inputs(seed: int = 0) -> dict:
    streams_of = jax.random.split(jax.random.key(seed), 14)
    return {
        "hidden_in": noise(streams_of[0], (ROWS, SEQ, D), 1.0, 6.0, ((0, 4), (1, 2))),
        "segments": draw_segments(jax.random.fold_in(streams_of[13], 71), 0),
        "positions": draw_positions(jax.random.fold_in(streams_of[13], 71), 0),
        "norm_gains": jnp.clip(1.0 + 0.18 * jax.random.normal(streams_of[3], (2, D), jnp.float32), 0.099609375, 1.8984375).astype(jnp.bfloat16),
        "norm_biases": noise(streams_of[4], (2, D), 0.3, 2.0, ((1, 4),)),
        "qkv_weight": noise(streams_of[5], (3, D, D), D ** -0.5, 0.21875, ((1, 4), (2, 4))),
        "qkv_bias": noise(streams_of[6], (3, HEADS, HD), 0.3, 2.0, ((1, 4), (2, 4))),
        "out_weight": noise(streams_of[7], (D, D), (D // 8) ** -0.5, 0.625, ((0, 4), (1, 4))),
        "up_weight": noise(streams_of[8], (D, FF), D ** -0.5, 0.21875, ((0, 4), (1, 4))),
        "up_bias": noise(streams_of[9], (FF // HD, HD), 0.3, 2.0, ((0, 4), (1, 4))),
        "down_weight": noise(streams_of[10], (FF, D), FF ** -0.5, 0.109375, ((0, 4), (1, 4))),
        "branch_biases": noise(streams_of[11], (2, D), 0.3, 2.0, ((1, 4),)),
        "out_grad": noise(streams_of[12], (ROWS, SEQ, D), 1.0, 6.0, ((0, 4), (1, 2))),
    }


@jax.custom_vjp
def low(v):
    return lax.optimization_barrier(v.astype(jnp.bfloat16)).astype(jnp.float32)

@jax.custom_vjp
def low_back(v):
    return v

def low_keep(v):
    return (low(v), None)

def low_pass(kept, grad):
    return (grad,)

def back_keep(v):
    return (v, None)

def back_low(kept, grad):
    return (low(grad),)
low.defvjp(low_keep, low_pass)
low_back.defvjp(back_keep, back_low)

def layer_scale(values, gain_row, shift_row):
    centred = values - lax.optimization_barrier(jnp.mean(values, axis=-1, keepdims=True))
    spread = lax.optimization_barrier(jnp.mean(centred * centred, axis=-1, keepdims=True))
    return centred * lax.rsqrt(spread + 1e-05) * gain_row + shift_row

def rotary(field_rows, cosine, sine_wave):
    rot_half = ROT // 2
    first_part = field_rows[..., :rot_half]
    second = field_rows[..., rot_half:ROT]
    return jnp.concatenate([first_part * cosine - second * sine_wave, second * cosine + first_part * sine_wave, field_rows[..., ROT:]], axis=-1)

def row_attention(row_items):
    query_rows, key_rows, value_rows, segment = row_items
    scores = jnp.einsum('qhe,khe->hqk', query_rows, key_rows, precision=lax.Precision.HIGHEST) * HD ** (-0.5)
    scores = low_back(scores)
    places = jnp.arange(SEQ)
    allowed = (segment[:, None] == segment[None, :]) & (places[None, :] <= places[:, None])
    scores = jnp.where(allowed[None], scores, -1e+30)
    row_top = lax.optimization_barrier(jnp.max(scores, axis=-1, keepdims=True))
    weights = jnp.exp(scores - row_top)
    probability = weights / lax.optimization_barrier(jnp.sum(weights, axis=-1, keepdims=True))
    mixed_rows = jnp.einsum('hqk,khe->qhe', low(probability), value_rows, precision=lax.Precision.HIGHEST)
    return mixed_rows.reshape(SEQ, D)

def forward(hidden, gains, shifts, w_qkv, b_qkv, w_out, w_up, b_up, w_down, b_branch, segments, positions):
    normed_attn = low(layer_scale(hidden, gains[0], shifts[0]))
    normed_mlp = low(layer_scale(hidden, gains[1], shifts[1]))
    projected = jnp.einsum('rsd,ide->irse', normed_attn, w_qkv, precision=lax.Precision.HIGHEST) + b_qkv.reshape(3, 1, 1, D)
    projected = low_back(projected).reshape(3, ROWS, SEQ, HEADS, HD)
    frequency = jnp.power(10000.0, -jnp.arange(0, ROT, 2).astype(jnp.float32) / ROT)
    angles = positions.astype(jnp.float32)[:, :, None, None] * frequency
    cosine = jnp.cos(angles)
    sine_wave = jnp.sin(angles)
    queries = low(rotary(projected[0], cosine, sine_wave))
    key_rows = low(rotary(projected[1], cosine, sine_wave))
    value_rows = low(projected[2])
    mixed_rows = lax.map(jax.checkpoint(row_attention), (queries, key_rows, value_rows, segments))
    mixed_rows = low(low_back(mixed_rows))
    attended = jnp.einsum('rse,ed->rsd', mixed_rows, w_out, precision=lax.Precision.HIGHEST)
    gated = low_back(jnp.einsum('rsd,df->rsf', normed_mlp, w_up, precision=lax.Precision.HIGHEST) + b_up.reshape(FF))
    activated = low(jax.nn.gelu(gated, approximate=False))
    expanded = jnp.einsum('rsf,fd->rsd', activated, w_down, precision=lax.Precision.HIGHEST)
    return hidden + attended + expanded + b_branch[0] + b_branch[1]

def reference(hidden_in, segments, positions, norm_gains, norm_biases, qkv_weight, qkv_bias, out_weight, up_weight, up_bias, down_weight, branch_biases, out_grad):
    floats = tuple((entry.astype(jnp.float32) for entry in (hidden_in, norm_gains, norm_biases, qkv_weight, qkv_bias, out_weight, up_weight, up_bias, down_weight, branch_biases)))

    def block_forward(*float_args):
        return forward(*float_args, segments, positions)
    result, pullback = jax.vjp(block_forward, *floats)
    gradients = pullback(out_grad.astype(jnp.float32))
    return (result.astype(jnp.bfloat16), gradients[0].astype(jnp.bfloat16), gradients[1], gradients[2], gradients[3], gradients[4], gradients[5], gradients[6], gradients[7], gradients[8], gradients[9])
```

```python
import functools
import math

import jax
import jax.numpy as jnp
from jax import lax
from jax.experimental import pallas as pl
from jax.experimental.pallas import tpu as pltpu
from jax.sharding import PartitionSpec as P

F32 = jnp.float32
BF16 = jnp.bfloat16
VMEM_BYTES = 56 * 1024 * 1024


def block_sizes(tokens):
    return min(256, tokens), min(512, tokens)


def to_rows(source, target, heads, head_dim, chunk):
    def one(step, _):
        at = pl.multiple_of(step * chunk, chunk)
        for h in range(heads):
            part = source[h * head_dim : (h + 1) * head_dim, pl.ds(at, chunk)]
            target[h, pl.ds(at, chunk), :] = part.astype(F32).T.astype(BF16)
        return 0

    lax.fori_loop(0, source.shape[1] // chunk, one, 0)


def allowed_keys(start_row, at_key, at_query, q_off, bk, bq):
    key = lax.broadcasted_iota(jnp.int32, (bk, bq), 0)
    query = lax.broadcasted_iota(jnp.int32, (1, bq), 1) + (at_query + q_off - at_key)
    return (key >= start_row - at_key) & (key <= query)


def forward_kernel(
    heads,
    head_dim,
    bq,
    bk,
    lo_ref,
    hi_ref,
    start_ref,
    q_ref,
    k0_ref,
    v0_ref,
    k1_ref,
    v1_ref,
    do_ref,
    out_ref,
    lse_ref,
    dot_ref,
    k_rows,
    v_cols,
    acc,
    top,
    total,
):
    tokens = q_ref.shape[1]

    def fill(source, offset):
        def one(step, _):
            at = pl.multiple_of(step * bk, bk)
            to = pl.multiple_of(step * bk + offset, bk)
            for h in range(heads):
                part = source[h * head_dim : (h + 1) * head_dim, pl.ds(at, bk)]
                k_rows[h, pl.ds(to, bk), :] = part.astype(F32).T.astype(BF16)
            return 0

        lax.fori_loop(0, tokens // bk, one, 0)

    fill(k0_ref, 0)
    fill(k1_ref, tokens)
    v_cols[:, :tokens] = v0_ref[...]
    v_cols[:, tokens:] = v1_ref[...]

    def query_block(b, _):
        at_query = pl.multiple_of(b * bq, bq)
        cols = pl.ds(at_query, bq)
        start_row = start_ref[:, cols]
        acc[...] = jnp.zeros_like(acc)
        top[...] = jnp.full_like(top, -1e30)
        total[...] = jnp.zeros_like(total)

        def key_block(kb, _):
            at_key = pl.multiple_of(kb * bk, bk)
            allowed = allowed_keys(start_row, at_key, at_query, tokens, bk, bq)
            for h in range(heads):
                rows = slice(h * head_dim, (h + 1) * head_dim)
                scores = jnp.dot(
                    k_rows[h, pl.ds(at_key, bk), :],
                    q_ref[rows, cols],
                    preferred_element_type=F32,
                )
                scores = jnp.where(allowed, scores, -1e30)
                old = top[h]
                new = jnp.maximum(old, jnp.max(scores, axis=0, keepdims=True))
                weights = jnp.exp(scores - new)
                shrink = jnp.exp(old - new)
                top[h] = new
                total[h] = total[h] * shrink + jnp.sum(weights, axis=0, keepdims=True)
                acc[h] = acc[h] * shrink + jnp.dot(
                    v_cols[rows, pl.ds(at_key, bk)],
                    weights.astype(BF16),
                    preferred_element_type=F32,
                )
            return 0

        lax.fori_loop(lo_ref[b], hi_ref[b], key_block, 0)
        for h in range(heads):
            rows = slice(h * head_dim, (h + 1) * head_dim)
            mixed = acc[h] / total[h]
            out_ref[rows, cols] = mixed.astype(BF16)
            lse_ref[h, :, cols] = top[h] + jnp.log(total[h])
            dot_ref[h, :, cols] = jnp.sum(
                mixed * do_ref[rows, cols].astype(F32), axis=0, keepdims=True
            )
        return 0

    lax.fori_loop(0, tokens // bq, query_block, 0)


def backward_kernel(
    heads,
    head_dim,
    bq,
    bk,
    q_off,
    lo_ref,
    hi_ref,
    start_ref,
    q_ref,
    do_ref,
    lse_ref,
    dot_ref,
    k_ref,
    v_ref,
    dq_ref,
    dk_ref,
    dv_ref,
    q_rows,
    do_rows,
    k_rows,
    v_rows,
    dk_acc,
    dv_acc,
):
    tokens = q_ref.shape[1]
    scale = head_dim**-0.5
    for source, target in ((q_ref, q_rows), (do_ref, do_rows), (k_ref, k_rows), (v_ref, v_rows)):
        to_rows(source, target, heads, head_dim, bk)
    dk_acc[...] = jnp.zeros_like(dk_acc)
    dv_acc[...] = jnp.zeros_like(dv_acc)
    dq_ref[...] = jnp.zeros_like(dq_ref)

    def query_block(b, _):
        at_query = pl.multiple_of(b * bq, bq)
        cols = pl.ds(at_query, bq)
        start_row = start_ref[:, cols]

        def key_block(kb, _):
            at_key = pl.multiple_of(kb * bk, bk)
            keys = pl.ds(at_key, bk)
            allowed = allowed_keys(start_row, at_key, at_query, q_off, bk, bq)
            for h in range(heads):
                rows = slice(h * head_dim, (h + 1) * head_dim)
                scores = jnp.dot(
                    k_rows[h, keys, :], q_ref[rows, cols], preferred_element_type=F32
                )
                prob = jnp.exp(jnp.where(allowed, scores - lse_ref[h, :, cols], -1e30))
                prob_grad = jnp.dot(
                    v_rows[h, keys, :], do_ref[rows, cols], preferred_element_type=F32
                )
                score_grad = (prob * (prob_grad - dot_ref[h, :, cols])).astype(BF16)
                dv_acc[h, keys, :] += jnp.dot(
                    prob.astype(BF16), do_rows[h, cols, :], preferred_element_type=F32
                )
                dk_acc[h, keys, :] += jnp.dot(
                    score_grad, q_rows[h, cols, :], preferred_element_type=F32
                )
                dq_ref[rows, cols] += jnp.dot(
                    k_ref[rows, keys], score_grad, preferred_element_type=F32
                )
            return 0

        lax.fori_loop(lo_ref[b], hi_ref[b], key_block, 0)
        dq_ref[:, cols] = dq_ref[:, cols] * scale
        return 0

    lax.fori_loop(0, tokens // bq, query_block, 0)

    def finish(step, _):
        at = pl.multiple_of(step * bk, bk)
        for h in range(heads):
            rows = slice(h * head_dim, (h + 1) * head_dim)
            dk_ref[rows, pl.ds(at, bk)] = dk_acc[h, pl.ds(at, bk), :].T.astype(dk_ref.dtype)
            dv_ref[rows, pl.ds(at, bk)] = dv_acc[h, pl.ds(at, bk), :].T.astype(dv_ref.dtype)
        return 0

    lax.fori_loop(0, tokens // bk, finish, 0)


def vmem(count):
    return [pl.BlockSpec(memory_space=pltpu.VMEM)] * count


def attention_forward(heads, head_dim, lo, hi, start, q, k0, v0, k1, v1, do):
    tokens = q.shape[1]
    bq, bk = block_sizes(tokens)
    width = heads * head_dim
    pairs = tokens * tokens * heads // 2
    return pl.pallas_call(
        functools.partial(forward_kernel, heads, head_dim, bq, bk),
        out_shape=(
            jax.ShapeDtypeStruct((width, tokens), BF16),
            jax.ShapeDtypeStruct((heads, 1, tokens), F32),
            jax.ShapeDtypeStruct((heads, 1, tokens), F32),
        ),
        in_specs=[pl.BlockSpec(memory_space=pltpu.SMEM)] * 2 + vmem(7),
        out_specs=tuple(vmem(3)),
        scratch_shapes=[
            pltpu.VMEM((heads, 2 * tokens, head_dim), BF16),
            pltpu.VMEM((width, 2 * tokens), BF16),
            pltpu.VMEM((heads, head_dim, bq), F32),
            pltpu.VMEM((heads, 1, bq), F32),
            pltpu.VMEM((heads, 1, bq), F32),
        ],
        compiler_params=pltpu.CompilerParams(vmem_limit_bytes=VMEM_BYTES),
        cost_estimate=pl.CostEstimate(
            flops=16 * pairs * head_dim, bytes_accessed=8 * width * tokens * 2, transcendentals=pairs
        ),
        name="attention_forward",
    )(lo, hi, start, q, k0, v0, k1, v1, do)


def attention_backward(heads, head_dim, q_off, kind, lo, hi, start, q, do, lse, dot, k, v):
    tokens = q.shape[1]
    bq, bk = block_sizes(tokens)
    width = heads * head_dim
    pairs = tokens * tokens * heads // 4
    return pl.pallas_call(
        functools.partial(backward_kernel, heads, head_dim, bq, bk, q_off),
        out_shape=(
            jax.ShapeDtypeStruct((width, tokens), F32),
            jax.ShapeDtypeStruct((width, tokens), kind),
            jax.ShapeDtypeStruct((width, tokens), kind),
        ),
        in_specs=[pl.BlockSpec(memory_space=pltpu.SMEM)] * 2 + vmem(7),
        out_specs=tuple(vmem(3)),
        scratch_shapes=[pltpu.VMEM((heads, tokens, head_dim), BF16)] * 4
        + [pltpu.VMEM((heads, tokens, head_dim), F32)] * 2,
        compiler_params=pltpu.CompilerParams(vmem_limit_bytes=VMEM_BYTES),
        cost_estimate=pl.CostEstimate(
            flops=40 * pairs * head_dim, bytes_accessed=8 * width * tokens * 2, transcendentals=pairs
        ),
        name="attention_cross_back" if q_off else "attention_own_back",
    )(lo, hi, start, q, do, lse, dot, k, v)


def rotate(field, cosine, sine_wave, direction, heads, head_dim):
    shaped = field.reshape(heads, head_dim, field.shape[1])
    half = head_dim // 8
    first, second = shaped[:, :half], shaped[:, half : 2 * half]
    turned = jnp.concatenate(
        [
            first * cosine - direction * second * sine_wave,
            second * cosine + direction * first * sine_wave,
            shaped[:, 2 * half :],
        ],
        axis=1,
    )
    return turned.reshape(field.shape)


def on_device(
    hidden_in,
    segments,
    positions,
    norm_gains,
    norm_biases,
    qkv_weight,
    qkv_bias,
    out_weight,
    up_weight,
    up_bias,
    down_weight,
    branch_biases,
    out_grad,
):
    rows, tokens, model = hidden_in.shape
    assert rows == 1
    fsdp = lax.axis_size("fsdp")
    ctx_size = lax.axis_size("ctx")
    tp = lax.axis_size("tp")
    ctx_index = lax.axis_index("ctx")
    heads, head_dim = qkv_bias.shape[1], qkv_bias.shape[2] * fsdp
    width = heads * head_dim
    hidden_units = up_weight.shape[1]

    w_qkv = lax.all_gather(qkv_weight, "fsdp", axis=1, tiled=True)
    small = jnp.concatenate(
        [
            part.reshape(-1, part.shape[-1])
            for part in (norm_gains, norm_biases, branch_biases)
        ],
        axis=0,
    )
    norms = lax.all_gather(small, "fsdp", axis=1, tiled=True).astype(F32)
    gains, shifts, branch_bias = norms[0:2], norms[2:4], norms[4:6]
    biases = jnp.concatenate([qkv_bias.reshape(-1, qkv_bias.shape[-1]), up_bias], axis=0)
    biases = lax.all_gather(biases, "fsdp", axis=1, tiled=True).astype(F32)
    b_qkv = biases[: 3 * heads].reshape(3, width)
    b_up = biases[3 * heads :].reshape(hidden_units)
    w_up = lax.all_gather(up_weight, "fsdp", axis=0, tiled=True)
    w_out = lax.all_gather(out_weight, "fsdp", axis=1, tiled=True)
    w_down = lax.all_gather(down_weight, "fsdp", axis=1, tiled=True)

    segs = segments.reshape(tokens)
    shift = [(i, i + 1) for i in range(ctx_size - 1)]
    back = [(i + 1, i) for i in range(ctx_size - 1)]
    earlier_segs = jnp.where(ctx_index == 0, -1, lax.ppermute(segs, "ctx", shift))
    segs_all = jnp.concatenate([earlier_segs, segs])
    start = jnp.sum((segs_all[:, None] < segs[None, :]).astype(jnp.int32), axis=0)
    bq, bk = block_sizes(tokens)
    blocks = tokens // bq
    start_block = start.reshape(blocks, bq)[:, 0]
    ends = (jnp.arange(blocks, dtype=jnp.int32) + 1) * bq
    own_hi = (ends + bk - 1) // bk
    fwd_lo, fwd_hi = start_block // bk, own_hi + tokens // bk
    own_lo = jnp.maximum(start_block - tokens, 0) // bk
    cross_hi = jnp.full((blocks,), tokens // bk, jnp.int32)
    cross_lo = jnp.minimum(start_block // bk, cross_hi)
    start_row = start.reshape(1, tokens)

    residual = hidden_in.reshape(tokens, model).astype(F32)
    centred = residual - jnp.mean(residual, axis=-1, keepdims=True)
    inv_spread = lax.rsqrt(jnp.mean(centred * centred, axis=-1, keepdims=True) + 1e-05)
    normal_unit = centred * inv_spread
    normed_attn = (normal_unit * gains[0] + shifts[0]).astype(BF16)
    normed_mlp = (normal_unit * gains[1] + shifts[1]).astype(BF16)
    projected = (
        jnp.einsum("nd,ide->ien", normed_attn, w_qkv, preferred_element_type=F32)
        + b_qkv[:, :, None]
    )
    rot_width = head_dim // 4
    frequency = jnp.power(10000.0, -jnp.arange(0, rot_width, 2).astype(F32) / rot_width)
    angles = positions.reshape(1, tokens).astype(F32) * frequency[:, None]
    cosine, sine_wave = jnp.cos(angles), jnp.sin(angles)
    score_scale = head_dim**-0.5
    q = rotate(projected[0], cosine, sine_wave, 1.0, heads, head_dim).astype(BF16)
    q = q * jnp.asarray(score_scale, BF16)
    k = rotate(projected[1], cosine, sine_wave, 1.0, heads, head_dim).astype(BF16)
    v = projected[2].astype(BF16)
    k0, v0 = lax.ppermute((k, v), "ctx", shift)

    grad_low = out_grad.reshape(tokens, model)
    up_pre = jnp.dot(normed_mlp, w_up, preferred_element_type=F32) + b_up
    cdf = 0.5 * (1.0 + lax.erf(up_pre * math.sqrt(0.5)))
    activated = (up_pre * cdf).astype(BF16)
    slope = (cdf + up_pre * (jnp.exp(-0.5 * up_pre * up_pre) * (1 / math.sqrt(2 * math.pi)))).astype(
        BF16
    )
    activated, slope = lax.optimization_barrier((activated, slope))
    expanded = jnp.dot(activated, w_down, preferred_element_type=F32)
    act_grad = jnp.einsum("nd,fd->nf", grad_low, w_down, preferred_element_type=F32)
    up_grad = (act_grad * slope.astype(F32)).astype(BF16)
    down_weight_part = jnp.einsum("nf,nd->fd", activated, grad_low, preferred_element_type=F32)
    up_weight_part = jnp.einsum("nd,nf->df", normed_mlp, up_grad, preferred_element_type=F32)
    up_bias_part = jnp.sum(up_grad, axis=0, dtype=F32)
    mlp_norm_grad = jnp.einsum("nf,df->nd", up_grad, w_up, preferred_element_type=F32)
    branch_row = jnp.sum(grad_low, axis=0, dtype=F32)

    def reduce_weight(part, axis):
        owned = lax.psum_scatter(part.astype(BF16), "fsdp", scatter_dimension=axis, tiled=True)
        return lax.psum(owned, "ctx").astype(F32)

    q, mlp_norm_grad, up_weight_part, down_weight_part, expanded = lax.optimization_barrier(
        (q, mlp_norm_grad.astype(BF16), up_weight_part.astype(BF16), down_weight_part.astype(BF16), expanded)
    )
    mlp_norm_grad = mlp_norm_grad.astype(F32)
    down_weight_grad = reduce_weight(down_weight_part, 1)
    up_weight_grad = reduce_weight(up_weight_part, 0)

    do = jnp.einsum("nd,ed->en", grad_low, w_out, preferred_element_type=F32).astype(BF16)
    mixed, lse, dot = attention_forward(
        heads, head_dim, fwd_lo, fwd_hi, start_row, q, k0, v0, k, v, do
    )
    attended = jnp.einsum("en,ed->nd", mixed, w_out, preferred_element_type=F32)
    branch_part, lse = lax.optimization_barrier(((attended + expanded).astype(BF16), lse))
    branch_total = lax.psum(branch_part, "tp")
    dq0, dk0, dv0 = attention_backward(
        heads, head_dim, tokens, BF16, cross_lo, cross_hi, start_row, q, do, lse, dot, k0, v0
    )
    dk_back, dv_back = lax.ppermute((dk0, dv0), "ctx", back)
    dq1, dk1, dv1 = attention_backward(
        heads, head_dim, 0, F32, own_lo, own_hi, start_row - tokens, q, do, lse, dot, k, v
    )
    out_weight_part = jnp.einsum("en,nd->ed", mixed, grad_low, preferred_element_type=F32)
    out_weight_grad = reduce_weight(out_weight_part, 1)

    branch_total, dq1 = lax.optimization_barrier((branch_total, dq1))
    hidden_out = (
        residual + branch_total.astype(F32) + branch_bias[0] + branch_bias[1]
    ).astype(BF16)
    projected_grad = jnp.stack(
        [
            rotate(dq0 + dq1, cosine, sine_wave, -1.0, heads, head_dim),
            rotate(dk1 + dk_back.astype(F32), cosine, sine_wave, -1.0, heads, head_dim),
            dv1 + dv_back.astype(F32),
        ]
    ).astype(BF16)
    attn_norm_grad = jnp.einsum("ien,ide->nd", projected_grad, w_qkv, preferred_element_type=F32)
    unit_part = (attn_norm_grad * gains[0] + mlp_norm_grad * gains[1]).astype(BF16)
    qkv_weight_part = jnp.einsum(
        "nd,ien->ide", normed_attn, projected_grad, preferred_element_type=F32
    )
    qkv_weight_grad = reduce_weight(qkv_weight_part, 1)
    qkv_bias_part = jnp.sum(projected_grad, axis=2, dtype=F32)

    tp_index = lax.axis_index("tp")
    everywhere = jnp.stack(
        [
            jnp.sum(attn_norm_grad * normal_unit, axis=0),
            jnp.sum(mlp_norm_grad * normal_unit, axis=0),
            jnp.sum(attn_norm_grad, axis=0),
            jnp.sum(mlp_norm_grad, axis=0),
            jnp.where(tp_index == 0, branch_row, 0.0),
        ]
    )
    own = jnp.concatenate([qkv_bias_part.reshape(-1), up_bias_part])
    slots = jnp.where(jnp.arange(tp)[:, None] == tp_index, own[None], 0.0)
    sums = lax.psum(
        jnp.concatenate([everywhere.reshape(-1), slots.reshape(-1)]), ("fsdp", "ctx", "tp")
    )
    unit_grad = lax.psum(unit_part, "tp")
    unit_grad, sums = lax.optimization_barrier((unit_grad, sums))
    unit_grad = unit_grad.astype(F32)
    input_sum = inv_spread * (
        unit_grad
        - jnp.mean(unit_grad, axis=-1, keepdims=True)
        - normal_unit * jnp.mean(unit_grad * normal_unit, axis=-1, keepdims=True)
    )
    input_grad = (grad_low.astype(F32) + input_sum).astype(BF16)
    norm_sums = sums[: 5 * model].reshape(5, model)
    own_sums = lax.dynamic_index_in_dim(
        sums[5 * model :].reshape(tp, -1), tp_index, axis=0, keepdims=False
    )
    fsdp_index = lax.axis_index("fsdp")

    def shard(whole):
        size = whole.shape[-1] // fsdp
        return lax.dynamic_slice_in_dim(whole, fsdp_index * size, size, axis=whole.ndim - 1)

    norm_sums = shard(norm_sums)
    qkv_bias_grad = shard(own_sums[: 3 * width].reshape(3, heads, head_dim))
    up_bias_grad = shard(own_sums[3 * width :].reshape(-1, head_dim))
    return (
        hidden_out.reshape(hidden_in.shape),
        input_grad.reshape(hidden_in.shape),
        norm_sums[0:2],
        norm_sums[2:4],
        qkv_weight_grad,
        qkv_bias_grad,
        out_weight_grad,
        up_weight_grad,
        up_bias_grad,
        down_weight_grad,
        jnp.stack([norm_sums[4], norm_sums[4]]),
    )


def solution(mesh):
    return jax.shard_map(
        on_device,
        mesh=mesh,
        in_specs=(
            P("fsdp", "ctx", None),
            P("fsdp", "ctx"),
            P("fsdp", "ctx"),
            P(None, "fsdp"),
            P(None, "fsdp"),
            P(None, "fsdp", "tp"),
            P(None, "tp", "fsdp"),
            P("tp", "fsdp"),
            P("fsdp", "tp"),
            P("tp", "fsdp"),
            P("tp", "fsdp"),
            P(None, "fsdp"),
            P("fsdp", "ctx", None),
        ),
        out_specs=(
            P("fsdp", "ctx", None),
            P("fsdp", "ctx", None),
            P(None, "fsdp"),
            P(None, "fsdp"),
            P(None, "fsdp", "tp"),
            P(None, "tp", "fsdp"),
            P("tp", "fsdp"),
            P("fsdp", "tp"),
            P("tp", "fsdp"),
            P("tp", "fsdp"),
            P(None, "fsdp"),
        ),
        check_vma=False,
    )
```

```python
import functools
import math

import jax
import jax.numpy as jnp
from jax import lax
from jax.experimental import pallas as pl
from jax.experimental.pallas import tpu as pltpu
from jax.sharding import PartitionSpec as P

F32 = jnp.float32
BF16 = jnp.bfloat16
VMEM_BYTES = 56 * 1024 * 1024


def block_sizes(tokens):
    return min(256, tokens), min(512, tokens)


def to_rows(source, first, target, heads, head_dim, chunk):
    def one(step, _):
        at = pl.multiple_of(step * chunk, chunk)
        for h in range(heads):
            part = source[first + h * head_dim : first + (h + 1) * head_dim, pl.ds(at, chunk)]
            target[h, pl.ds(at, chunk), :] = part.astype(F32).T.astype(BF16)
        return 0

    lax.fori_loop(0, source.shape[1] // chunk, one, 0)


def allowed_keys(start_row, at_key, at_query, q_off, bk, bq):
    key = lax.broadcasted_iota(jnp.int32, (bk, bq), 0)
    query = lax.broadcasted_iota(jnp.int32, (1, bq), 1) + (at_query + q_off - at_key)
    return (key >= start_row - at_key) & (key <= query)


def forward_kernel(
    heads,
    head_dim,
    bq,
    bk,
    lo_ref,
    hi_ref,
    start_ref,
    q_ref,
    kv0_ref,
    kv1_ref,
    do_ref,
    out_ref,
    lse_ref,
    dot_ref,
    k_rows,
    v_cols,
    acc,
    top,
    total,
):
    tokens = q_ref.shape[1]
    width = heads * head_dim

    def fill(source, offset):
        def one(step, _):
            at = pl.multiple_of(step * bk, bk)
            to = pl.multiple_of(step * bk + offset, bk)
            for h in range(heads):
                part = source[h * head_dim : (h + 1) * head_dim, pl.ds(at, bk)]
                k_rows[h, pl.ds(to, bk), :] = part.astype(F32).T.astype(BF16)
            return 0

        lax.fori_loop(0, tokens // bk, one, 0)

    fill(kv0_ref, 0)
    fill(kv1_ref, tokens)
    v_cols[:, :tokens] = kv0_ref[width:, :]
    v_cols[:, tokens:] = kv1_ref[width:, :]

    def query_block(b, _):
        at_query = pl.multiple_of(b * bq, bq)
        cols = pl.ds(at_query, bq)
        start_row = start_ref[:, cols]
        acc[...] = jnp.zeros_like(acc)
        top[...] = jnp.full_like(top, -1e30)
        total[...] = jnp.zeros_like(total)

        def key_block(kb, _):
            at_key = pl.multiple_of(kb * bk, bk)
            allowed = allowed_keys(start_row, at_key, at_query, tokens, bk, bq)
            for h in range(heads):
                rows = slice(h * head_dim, (h + 1) * head_dim)
                scores = jnp.dot(
                    k_rows[h, pl.ds(at_key, bk), :],
                    q_ref[rows, cols],
                    preferred_element_type=F32,
                )
                scores = jnp.where(allowed, scores, -1e30)
                old = top[h]
                new = jnp.maximum(old, jnp.max(scores, axis=0, keepdims=True))
                weights = jnp.exp(scores - new)
                shrink = jnp.exp(old - new)
                top[h] = new
                total[h] = total[h] * shrink + jnp.sum(weights, axis=0, keepdims=True)
                acc[h] = acc[h] * shrink + jnp.dot(
                    v_cols[rows, pl.ds(at_key, bk)],
                    weights.astype(BF16),
                    preferred_element_type=F32,
                )
            return 0

        lax.fori_loop(lo_ref[b], hi_ref[b], key_block, 0)
        for h in range(heads):
            rows = slice(h * head_dim, (h + 1) * head_dim)
            mixed = acc[h] / total[h]
            out_ref[rows, cols] = mixed.astype(BF16)
            lse_ref[h, :, cols] = top[h] + jnp.log(total[h])
            dot_ref[h, :, cols] = jnp.sum(
                mixed * do_ref[rows, cols].astype(F32), axis=0, keepdims=True
            )
        return 0

    lax.fori_loop(0, tokens // bq, query_block, 0)


def backward_kernel(
    heads,
    head_dim,
    bq,
    bk,
    q_off,
    lo_ref,
    hi_ref,
    start_ref,
    q_ref,
    do_ref,
    lse_ref,
    dot_ref,
    kv_ref,
    dq_ref,
    dkv_ref,
    q_rows,
    do_rows,
    k_rows,
    v_rows,
    dk_acc,
    dv_acc,
):
    tokens = q_ref.shape[1]
    width = heads * head_dim
    scale = head_dim**-0.5
    for source, first, target in (
        (q_ref, 0, q_rows),
        (do_ref, 0, do_rows),
        (kv_ref, 0, k_rows),
        (kv_ref, width, v_rows),
    ):
        to_rows(source, first, target, heads, head_dim, bk)
    dk_acc[...] = jnp.zeros_like(dk_acc)
    dv_acc[...] = jnp.zeros_like(dv_acc)
    dq_ref[...] = jnp.zeros_like(dq_ref)

    def query_block(b, _):
        at_query = pl.multiple_of(b * bq, bq)
        cols = pl.ds(at_query, bq)
        start_row = start_ref[:, cols]

        def key_block(kb, _):
            at_key = pl.multiple_of(kb * bk, bk)
            keys = pl.ds(at_key, bk)
            allowed = allowed_keys(start_row, at_key, at_query, q_off, bk, bq)
            for h in range(heads):
                rows = slice(h * head_dim, (h + 1) * head_dim)
                scores = jnp.dot(
                    k_rows[h, keys, :], q_ref[rows, cols], preferred_element_type=F32
                )
                prob = jnp.exp(jnp.where(allowed, scores - lse_ref[h, :, cols], -1e30))
                prob_grad = jnp.dot(
                    v_rows[h, keys, :], do_ref[rows, cols], preferred_element_type=F32
                )
                score_grad = (prob * (prob_grad - dot_ref[h, :, cols])).astype(BF16)
                dv_acc[h, keys, :] += jnp.dot(
                    prob.astype(BF16), do_rows[h, cols, :], preferred_element_type=F32
                )
                dk_acc[h, keys, :] += jnp.dot(
                    score_grad, q_rows[h, cols, :], preferred_element_type=F32
                )
                dq_ref[rows, cols] += jnp.dot(
                    kv_ref[rows, keys], score_grad, preferred_element_type=F32
                )
            return 0

        lax.fori_loop(lo_ref[b], hi_ref[b], key_block, 0)
        dq_ref[:, cols] = dq_ref[:, cols] * scale
        return 0

    lax.fori_loop(0, tokens // bq, query_block, 0)

    def finish(step, _):
        at = pl.multiple_of(step * bk, bk)
        for h in range(heads):
            rows = slice(h * head_dim, (h + 1) * head_dim)
            low = slice(width + h * head_dim, width + (h + 1) * head_dim)
            dkv_ref[rows, pl.ds(at, bk)] = dk_acc[h, pl.ds(at, bk), :].T.astype(dkv_ref.dtype)
            dkv_ref[low, pl.ds(at, bk)] = dv_acc[h, pl.ds(at, bk), :].T.astype(dkv_ref.dtype)
        return 0

    lax.fori_loop(0, tokens // bk, finish, 0)


def vmem(count):
    return [pl.BlockSpec(memory_space=pltpu.VMEM)] * count


def attention_forward(heads, head_dim, lo, hi, start, q, kv0, kv1, do):
    tokens = q.shape[1]
    bq, bk = block_sizes(tokens)
    width = heads * head_dim
    return pl.pallas_call(
        functools.partial(forward_kernel, heads, head_dim, bq, bk),
        out_shape=(
            jax.ShapeDtypeStruct((width, tokens), BF16),
            jax.ShapeDtypeStruct((heads, 1, tokens), F32),
            jax.ShapeDtypeStruct((heads, 1, tokens), F32),
        ),
        in_specs=[pl.BlockSpec(memory_space=pltpu.SMEM)] * 2 + vmem(5),
        out_specs=tuple(vmem(3)),
        scratch_shapes=[
            pltpu.VMEM((heads, 2 * tokens, head_dim), BF16),
            pltpu.VMEM((width, 2 * tokens), BF16),
            pltpu.VMEM((heads, head_dim, bq), F32),
            pltpu.VMEM((heads, 1, bq), F32),
            pltpu.VMEM((heads, 1, bq), F32),
        ],
        compiler_params=pltpu.CompilerParams(vmem_limit_bytes=VMEM_BYTES),
        cost_estimate=pl.CostEstimate(
            flops=0, bytes_accessed=8 * width * tokens * 2, transcendentals=0
        ),
        name="attention_forward",
    )(lo, hi, start, q, kv0, kv1, do)


def attention_backward(heads, head_dim, q_off, kind, lo, hi, start, q, do, lse, dot, kv):
    tokens = q.shape[1]
    bq, bk = block_sizes(tokens)
    width = heads * head_dim
    return pl.pallas_call(
        functools.partial(backward_kernel, heads, head_dim, bq, bk, q_off),
        out_shape=(
            jax.ShapeDtypeStruct((width, tokens), F32),
            jax.ShapeDtypeStruct((2 * width, tokens), kind),
        ),
        in_specs=[pl.BlockSpec(memory_space=pltpu.SMEM)] * 2 + vmem(6),
        out_specs=tuple(vmem(2)),
        scratch_shapes=[pltpu.VMEM((heads, tokens, head_dim), BF16)] * 4
        + [pltpu.VMEM((heads, tokens, head_dim), F32)] * 2,
        compiler_params=pltpu.CompilerParams(vmem_limit_bytes=VMEM_BYTES),
        cost_estimate=pl.CostEstimate(
            flops=0, bytes_accessed=8 * width * tokens * 2, transcendentals=0
        ),
        name="attention_cross_back" if q_off else "attention_own_back",
    )(lo, hi, start, q, do, lse, dot, kv)


def rotate(field, cosine, sine_wave, direction, heads, head_dim):
    shaped = field.reshape(heads, head_dim, field.shape[1])
    half = head_dim // 8
    first, second = shaped[:, :half], shaped[:, half : 2 * half]
    turned = jnp.concatenate(
        [
            first * cosine - direction * second * sine_wave,
            second * cosine + direction * first * sine_wave,
            shaped[:, 2 * half :],
        ],
        axis=1,
    )
    return turned.reshape(field.shape)


def axis_swap(value, axis, bit):
    size = lax.axis_size(axis)
    return lax.ppermute(value, axis, [(i, i ^ bit) for i in range(size)])


def sum_pairs(value, axis):
    size = lax.axis_size(axis)
    if size & (size - 1):
        return lax.psum(value, axis)
    bit = 1
    while bit < size:
        value = value + axis_swap(value, axis, bit)
        bit *= 2
    return value


def gather_rows(part, after=()):
    peers = lax.axis_size("fsdp")
    if peers > 4:
        return lax.all_gather(part, "fsdp", axis=0, tiled=True)
    me, rows = lax.axis_index("fsdp"), part.shape[0]
    whole = jnp.zeros((peers * rows, part.shape[1]), part.dtype)
    for by in range(peers):
        if by == 0:
            piece, _ = lax.optimization_barrier((part, after))
        else:
            piece = lax.ppermute(part, "fsdp", [(i, (i + by) % peers) for i in range(peers)])
        whole = lax.dynamic_update_slice_in_dim(whole, piece, ((me - by) % peers) * rows, 0)
    return whole


def scatter_rows(part, after=()):
    peers = lax.axis_size("fsdp")
    if peers > 4:
        total = lax.psum_scatter(part, "fsdp", scatter_dimension=0, tiled=True).astype(F32)
    else:
        me, rows = lax.axis_index("fsdp"), part.shape[0] // peers
        own, _ = lax.optimization_barrier(
            (lax.dynamic_slice_in_dim(part, me * rows, rows, 0), after)
        )
        total = own.astype(F32)
        for by in range(1, peers):
            send = lax.dynamic_slice_in_dim(part, ((me + by) % peers) * rows, rows, 0)
            got = lax.ppermute(send, "fsdp", [(i, (i + by) % peers) for i in range(peers)])
            total = total + got.astype(F32)
    low = lax.optimization_barrier(total.astype(BF16))
    if lax.axis_size("ctx") != 2:
        return lax.psum(low, "ctx").astype(F32)
    return low.astype(F32) + axis_swap(low, "ctx", 1).astype(F32)


def tp_half(whole):
    core = lax.axis_index("tp") % 2
    rows = whole.shape[0] // 2
    return (
        lax.dynamic_slice_in_dim(whole, core * rows, rows, 0),
        lax.dynamic_slice_in_dim(whole, (1 - core) * rows, rows, 0),
    )


def tp_sum_core(part):
    mine, other = tp_half(part)
    half = mine.astype(F32) + axis_swap(other, "tp", 1).astype(F32)
    return lax.optimization_barrier(half.astype(BF16))


def tp_sum_chips(low, after=()):
    own, _ = lax.optimization_barrier((low, after))
    half = own.astype(F32)
    bit = 2
    while bit < lax.axis_size("tp"):
        if bit > 2:
            low = lax.optimization_barrier(half.astype(BF16))
            half = low.astype(F32)
        half = half + axis_swap(low, "tp", bit).astype(F32)
        bit *= 2
    return half


def tp_join(half):
    half = lax.optimization_barrier(half)
    other = axis_swap(half, "tp", 1)
    first = lax.axis_index("tp") % 2 == 0
    return [jnp.where(first, half, other), jnp.where(first, other, half)]


def on_device(
    hidden_in,
    segments,
    positions,
    norm_gains,
    norm_biases,
    qkv_weight,
    qkv_bias,
    out_weight,
    up_weight,
    up_bias,
    down_weight,
    branch_biases,
    out_grad,
):
    rows, tokens, model = hidden_in.shape
    assert rows == 1
    fsdp = lax.axis_size("fsdp")
    ctx_size = lax.axis_size("ctx")
    tp = lax.axis_size("tp")
    ctx_index = lax.axis_index("ctx")
    heads, head_dim = qkv_bias.shape[1], qkv_bias.shape[2] * fsdp
    width = heads * head_dim
    hidden_units = up_weight.shape[1]
    shard_rows = qkv_weight.shape[1]
    barrier = lax.optimization_barrier

    segs = segments.reshape(tokens)
    shift = [(i, i + 1) for i in range(ctx_size - 1)]
    back = [(i + 1, i) for i in range(ctx_size - 1)]
    earlier_segs = lax.ppermute(segs, "ctx", shift)
    small = [norm_gains, norm_biases, branch_biases, qkv_bias, up_bias]
    small = jnp.concatenate([part.reshape(-1) for part in small])
    extra = -(-small.size // (48 * width)) * 16
    small_count = small.size
    small = jnp.pad(small, (0, extra * 3 * width - small.size)).reshape(extra, 3 * width)
    first = jnp.transpose(qkv_weight, (1, 0, 2)).reshape(shard_rows, 3 * width)
    first = gather_rows(jnp.concatenate([first, small], axis=0))
    first = first.reshape(fsdp, shard_rows + extra, 3 * width)
    w_qkv = first[:, :shard_rows].reshape(model, 3 * width)
    small = first[:, shard_rows:].reshape(fsdp, -1)[:, :small_count]
    norm_count = 6 * shard_rows
    norms = small[:, :norm_count].astype(F32).reshape(fsdp, 6, shard_rows)
    norms = jnp.transpose(norms, (1, 0, 2)).reshape(6, model)
    gains, shifts, branch_bias = norms[0:2], norms[2:4], norms[4:6]
    biases = small[:, norm_count:].astype(F32).reshape(fsdp, -1, head_dim // fsdp)
    biases = jnp.transpose(biases, (1, 0, 2)).reshape(-1)
    b_qkv, b_up = biases[: 3 * width], biases[3 * width :]
    second = jnp.concatenate([up_weight, out_weight.T], axis=1)
    w_qkv, second = barrier((w_qkv, second))
    second = gather_rows(second)
    third, second = barrier((down_weight.T, second))
    w_up, w_out = second[:, :hidden_units], second[:, hidden_units:]

    earlier_segs = jnp.where(ctx_index == 0, -1, earlier_segs)
    segs_all = jnp.concatenate([earlier_segs, segs])
    start = jnp.sum((segs_all[:, None] < segs[None, :]).astype(jnp.int32), axis=0)
    bq, bk = block_sizes(tokens)
    blocks = tokens // bq
    start_block = start.reshape(blocks, bq)[:, 0]
    ends = (jnp.arange(blocks, dtype=jnp.int32) + 1) * bq
    own_hi = (ends + bk - 1) // bk
    fwd_lo, fwd_hi = start_block // bk, own_hi + tokens // bk
    own_lo = jnp.maximum(start_block - tokens, 0) // bk
    cross_hi = jnp.full((blocks,), tokens // bk, jnp.int32)
    cross_lo = jnp.minimum(start_block // bk, cross_hi)
    start_row = start.reshape(1, tokens)

    residual = hidden_in.reshape(tokens, model).astype(F32)
    centred = residual - jnp.mean(residual, axis=-1, keepdims=True)
    inv_spread = lax.rsqrt(jnp.mean(centred * centred, axis=-1, keepdims=True) + 1e-05)
    normal_unit = centred * inv_spread
    normed_attn = (normal_unit * gains[0] + shifts[0]).astype(BF16)
    normed_mlp = (normal_unit * gains[1] + shifts[1]).astype(BF16)
    projected = (
        jnp.einsum("nd,de->en", normed_attn, w_qkv, preferred_element_type=F32) + b_qkv[:, None]
    )
    rot_width = head_dim // 4
    frequency = jnp.power(10000.0, -jnp.arange(0, rot_width, 2).astype(F32) / rot_width)
    angles = positions.reshape(1, tokens).astype(F32) * frequency[:, None]
    cosine, sine_wave = jnp.cos(angles), jnp.sin(angles)
    score_scale = head_dim**-0.5
    q = rotate(projected[:width], cosine, sine_wave, 1.0, heads, head_dim).astype(BF16)
    q = q * jnp.asarray(score_scale, BF16)
    k = rotate(projected[width : 2 * width], cosine, sine_wave, 1.0, heads, head_dim)
    kv = jnp.concatenate([k, projected[2 * width :]], axis=0).astype(BF16)
    kv0 = lax.ppermute(kv, "ctx", shift)

    grad_low = out_grad.reshape(tokens, model)
    up_pre = jnp.dot(normed_mlp, w_up, preferred_element_type=F32) + b_up
    cdf = 0.5 * (1.0 + lax.erf(up_pre * math.sqrt(0.5)))
    activated = (up_pre * cdf).astype(BF16)
    slope = (cdf + up_pre * (jnp.exp(-0.5 * up_pre * up_pre) * (1 / math.sqrt(2 * math.pi)))).astype(
        BF16
    )
    do = jnp.einsum("nd,de->en", grad_low, w_out, preferred_element_type=F32).astype(BF16)
    activated, slope, do = barrier((activated, slope, do))
    mixed, lse, dot = attention_forward(
        heads, head_dim, fwd_lo, fwd_hi, start_row, q, kv0, kv, do
    )

    w_down = gather_rows(third, mixed)
    activated, mixed = barrier((activated, mixed))
    branch_part = jnp.einsum("en,de->nd", mixed, w_out, preferred_element_type=F32) + jnp.einsum(
        "nf,df->nd", activated, w_down, preferred_element_type=F32
    )
    down_part = jnp.einsum("nd,nf->df", grad_low, activated, preferred_element_type=F32)
    branch_part, down_part, lse = barrier((branch_part.astype(BF16), down_part.astype(BF16), lse))
    branch_low, lse = barrier((tp_sum_core(branch_part), lse))
    dq0, dkv0 = attention_backward(
        heads, head_dim, tokens, BF16, cross_lo, cross_hi, start_row, q, do, lse, dot, kv0
    )
    dkv_back = lax.ppermute(dkv0, "ctx", back)

    slope, dq0 = barrier((slope, dq0))
    act_grad = jnp.einsum("nd,df->nf", grad_low, w_down, preferred_element_type=F32)
    up_grad = barrier((act_grad * slope.astype(F32)).astype(BF16))
    up_part = jnp.einsum("nd,nf->df", normed_mlp, up_grad, preferred_element_type=F32)
    mlp_norm_grad = jnp.einsum("nf,df->nd", up_grad, w_up, preferred_element_type=F32)
    up_bias_part = jnp.sum(up_grad, axis=0, dtype=F32)
    branch_row = jnp.sum(grad_low, axis=0, dtype=F32)
    out_part = jnp.einsum("nd,en->de", grad_low, mixed, preferred_element_type=F32)
    up_part, out_part, lse = barrier((up_part.astype(BF16), out_part.astype(BF16), lse))
    branch_half = tp_sum_chips(branch_low, up_part)
    down_weight_grad = scatter_rows(down_part, up_part)
    up_part, down_weight_grad, branch_half, lse = barrier(
        (up_part, down_weight_grad, branch_half, lse)
    )
    down_weight_grad = down_weight_grad.T
    dq1, dkv1 = attention_backward(
        heads, head_dim, 0, F32, own_lo, own_hi, start_row - tokens, q, do, lse, dot, kv
    )
    up_weight_grad = scatter_rows(up_part, dq1)
    residual_half, _ = tp_half(hidden_in.reshape(tokens, model))
    hidden_half = (
        residual_half.astype(F32) + branch_half + branch_bias[0] + branch_bias[1]
    ).astype(BF16)
    hidden_out = jnp.concatenate(tp_join(hidden_half), axis=0)

    dkv = dkv1 + dkv_back.astype(F32)
    projected_grad = jnp.concatenate(
        [
            rotate(dq0 + dq1, cosine, sine_wave, -1.0, heads, head_dim),
            rotate(dkv[:width], cosine, sine_wave, -1.0, heads, head_dim),
            dkv[width:],
        ],
        axis=0,
    ).astype(BF16)
    projected_grad = barrier(projected_grad)

    chunk = tokens // 2
    input_halves = []
    parts = []
    for c in range(2):
        cut = slice(c * chunk, (c + 1) * chunk)
        attn_norm_grad = jnp.einsum(
            "en,de->nd", projected_grad[:, cut], w_qkv, preferred_element_type=F32
        )
        unit_part = attn_norm_grad * gains[0] + mlp_norm_grad[cut] * gains[1]
        parts.append((tp_sum_core(barrier(unit_part.astype(BF16))), attn_norm_grad))
    low0, low1, projected_grad = barrier((parts[0][0], parts[1][0], projected_grad))
    attn_norm_grad = jnp.concatenate([parts[0][1], parts[1][1]], axis=0)
    qkv_part = jnp.einsum("nd,en->de", normed_attn, projected_grad, preferred_element_type=F32)
    last_part = jnp.concatenate([qkv_part.astype(BF16), out_part], axis=1)
    qkv_bias_part = jnp.sum(projected_grad, axis=1, dtype=F32)

    tp_index = lax.axis_index("tp")
    everywhere = jnp.concatenate(
        [
            jnp.sum(attn_norm_grad * normal_unit, axis=0),
            jnp.sum(mlp_norm_grad * normal_unit, axis=0),
            jnp.sum(attn_norm_grad, axis=0),
            jnp.sum(mlp_norm_grad, axis=0),
            jnp.where(tp_index == 0, branch_row, 0.0),
        ]
    )
    own = jnp.concatenate([qkv_bias_part, up_bias_part])
    slots = jnp.where(jnp.arange(tp)[:, None] == tp_index, own[None], 0.0)
    sums = jnp.concatenate([everywhere, slots.reshape(-1)])
    unit_first, last_part, sums = barrier(
        (tp_sum_chips(low0, (last_part, sums)), last_part, sums)
    )
    for c in range(2):
        cut = slice(c * chunk, (c + 1) * chunk)
        unit_grad = tp_sum_chips(low1) if c else unit_first
        hidden_part, _ = tp_half(hidden_in.reshape(tokens, model)[cut])
        residual_part = hidden_part.astype(F32)
        centred_part = residual_part - jnp.mean(residual_part, axis=-1, keepdims=True)
        spread_part = lax.rsqrt(
            jnp.mean(centred_part * centred_part, axis=-1, keepdims=True) + 1e-05
        )
        unit = centred_part * spread_part
        grad_part, _ = tp_half(grad_low[cut])
        input_half = grad_part.astype(F32) + spread_part * (
            unit_grad
            - jnp.mean(unit_grad, axis=-1, keepdims=True)
            - unit * jnp.mean(unit_grad * unit, axis=-1, keepdims=True)
        )
        input_halves += tp_join(input_half.astype(BF16))
    input_grad = jnp.concatenate(input_halves, axis=0)
    last_grad = scatter_rows(last_part)
    qkv_weight_grad = jnp.transpose(
        last_grad[:, : 3 * width].reshape(shard_rows, 3, width), (1, 0, 2)
    )
    out_weight_grad = last_grad[:, 3 * width :].T
    for axis in ("tp", "ctx", "fsdp"):
        sums = sum_pairs(sums, axis)
    norm_sums = sums[: 5 * model].reshape(5, model)
    own_sums = lax.dynamic_index_in_dim(
        sums[5 * model :].reshape(tp, -1), tp_index, axis=0, keepdims=False
    )
    fsdp_index = lax.axis_index("fsdp")

    def shard(whole):
        size = whole.shape[-1] // fsdp
        return lax.dynamic_slice_in_dim(whole, fsdp_index * size, size, axis=whole.ndim - 1)

    norm_sums = shard(norm_sums)
    qkv_bias_grad = shard(own_sums[: 3 * width].reshape(3, heads, head_dim))
    up_bias_grad = shard(own_sums[3 * width :].reshape(-1, head_dim))
    return (
        hidden_out.reshape(hidden_in.shape),
        input_grad.reshape(hidden_in.shape),
        norm_sums[0:2],
        norm_sums[2:4],
        qkv_weight_grad,
        qkv_bias_grad,
        out_weight_grad,
        up_weight_grad,
        up_bias_grad,
        down_weight_grad,
        jnp.stack([norm_sums[4], norm_sums[4]]),
    )


def solution(mesh):
    return jax.shard_map(
        on_device,
        mesh=mesh,
        in_specs=(
            P("fsdp", "ctx", None),
            P("fsdp", "ctx"),
            P("fsdp", "ctx"),
            P(None, "fsdp"),
            P(None, "fsdp"),
            P(None, "fsdp", "tp"),
            P(None, "tp", "fsdp"),
            P("tp", "fsdp"),
            P("fsdp", "tp"),
            P("tp", "fsdp"),
            P("tp", "fsdp"),
            P(None, "fsdp"),
            P("fsdp", "ctx", None),
        ),
        out_specs=(
            P("fsdp", "ctx", None),
            P("fsdp", "ctx", None),
            P(None, "fsdp"),
            P(None, "fsdp"),
            P(None, "fsdp", "tp"),
            P(None, "tp", "fsdp"),
            P("tp", "fsdp"),
            P("fsdp", "tp"),
            P("tp", "fsdp"),
            P("tp", "fsdp"),
            P(None, "fsdp"),
        ),
        check_vma=False,
    )
```

```python
import functools
import math

import jax
import jax.numpy as jnp
from jax import lax
from jax.experimental import pallas as pl
from jax.experimental.pallas import tpu as pltpu
from jax.sharding import PartitionSpec as P

F32 = jnp.float32
BF16 = jnp.bfloat16
VMEM_BYTES = 56 * 1024 * 1024


def block_sizes(tokens):
    return min(256, tokens), min(512, tokens)


def to_rows(source, first, target, heads, head_dim, chunk):
    def one(step, _):
        at = pl.multiple_of(step * chunk, chunk)
        for h in range(heads):
            part = source[first + h * head_dim : first + (h + 1) * head_dim, pl.ds(at, chunk)]
            target[h, pl.ds(at, chunk), :] = part.astype(F32).T.astype(BF16)
        return 0

    lax.fori_loop(0, source.shape[1] // chunk, one, 0)


def allowed_keys(start_row, at_key, at_query, q_off, bk, bq):
    key = lax.broadcasted_iota(jnp.int32, (bk, bq), 0)
    query = lax.broadcasted_iota(jnp.int32, (1, bq), 1) + (at_query + q_off - at_key)
    return (key >= start_row - at_key) & (key <= query)


def forward_kernel(
    heads,
    head_dim,
    bq,
    bk,
    lo_ref,
    hi_ref,
    start_ref,
    q_ref,
    kv0_ref,
    kv1_ref,
    do_ref,
    out_ref,
    lse_ref,
    dot_ref,
    k_rows,
    v_cols,
    acc,
    top,
    total,
):
    tokens = q_ref.shape[1]
    width = heads * head_dim

    def fill(source, offset):
        def one(step, _):
            at = pl.multiple_of(step * bk, bk)
            to = pl.multiple_of(step * bk + offset, bk)
            for h in range(heads):
                part = source[h * head_dim : (h + 1) * head_dim, pl.ds(at, bk)]
                k_rows[h, pl.ds(to, bk), :] = part.astype(F32).T.astype(BF16)
            return 0

        lax.fori_loop(0, tokens // bk, one, 0)

    fill(kv0_ref, 0)
    fill(kv1_ref, tokens)
    v_cols[:, :tokens] = kv0_ref[width:, :]
    v_cols[:, tokens:] = kv1_ref[width:, :]

    def query_block(b, _):
        at_query = pl.multiple_of(b * bq, bq)
        cols = pl.ds(at_query, bq)
        start_row = start_ref[:, cols]
        acc[...] = jnp.zeros_like(acc)
        top[...] = jnp.full_like(top, -1e30)
        total[...] = jnp.zeros_like(total)

        def key_block(kb, _):
            at_key = pl.multiple_of(kb * bk, bk)
            allowed = allowed_keys(start_row, at_key, at_query, tokens, bk, bq)
            for h in range(heads):
                rows = slice(h * head_dim, (h + 1) * head_dim)
                scores = jnp.dot(
                    k_rows[h, pl.ds(at_key, bk), :],
                    q_ref[rows, cols],
                    preferred_element_type=F32,
                )
                scores = jnp.where(allowed, scores, -1e30)
                old = top[h]
                new = jnp.maximum(old, jnp.max(scores, axis=0, keepdims=True))
                weights = jnp.exp(scores - new)
                shrink = jnp.exp(old - new)
                top[h] = new
                total[h] = total[h] * shrink + jnp.sum(weights, axis=0, keepdims=True)
                acc[h] = acc[h] * shrink + jnp.dot(
                    v_cols[rows, pl.ds(at_key, bk)],
                    weights.astype(BF16),
                    preferred_element_type=F32,
                )
            return 0

        lax.fori_loop(lo_ref[b], hi_ref[b], key_block, 0)
        for h in range(heads):
            rows = slice(h * head_dim, (h + 1) * head_dim)
            mixed = acc[h] / total[h]
            out_ref[rows, cols] = mixed.astype(BF16)
            lse_ref[h, :, cols] = top[h] + jnp.log(total[h])
            dot_ref[h, :, cols] = jnp.sum(
                mixed * do_ref[rows, cols].astype(F32), axis=0, keepdims=True
            )
        return 0

    lax.fori_loop(0, tokens // bq, query_block, 0)


def backward_kernel(
    heads,
    head_dim,
    bq,
    bk,
    q_off,
    lo_ref,
    hi_ref,
    start_ref,
    q_ref,
    do_ref,
    lse_ref,
    dot_ref,
    kv_ref,
    dq_ref,
    dkv_ref,
    q_rows,
    do_rows,
    k_rows,
    v_rows,
    dk_acc,
    dv_acc,
):
    tokens = q_ref.shape[1]
    width = heads * head_dim
    scale = head_dim**-0.5
    for source, first, target in (
        (q_ref, 0, q_rows),
        (do_ref, 0, do_rows),
        (kv_ref, 0, k_rows),
        (kv_ref, width, v_rows),
    ):
        to_rows(source, first, target, heads, head_dim, bk)
    dk_acc[...] = jnp.zeros_like(dk_acc)
    dv_acc[...] = jnp.zeros_like(dv_acc)
    dq_ref[...] = jnp.zeros_like(dq_ref)

    def query_block(b, _):
        at_query = pl.multiple_of(b * bq, bq)
        cols = pl.ds(at_query, bq)
        start_row = start_ref[:, cols]

        def key_block(kb, _):
            at_key = pl.multiple_of(kb * bk, bk)
            keys = pl.ds(at_key, bk)
            allowed = allowed_keys(start_row, at_key, at_query, q_off, bk, bq)
            for h in range(heads):
                rows = slice(h * head_dim, (h + 1) * head_dim)
                scores = jnp.dot(
                    k_rows[h, keys, :], q_ref[rows, cols], preferred_element_type=F32
                )
                prob = jnp.exp(jnp.where(allowed, scores - lse_ref[h, :, cols], -1e30))
                prob_grad = jnp.dot(
                    v_rows[h, keys, :], do_ref[rows, cols], preferred_element_type=F32
                )
                score_grad = (prob * (prob_grad - dot_ref[h, :, cols])).astype(BF16)
                dv_acc[h, keys, :] += jnp.dot(
                    prob.astype(BF16), do_rows[h, cols, :], preferred_element_type=F32
                )
                dk_acc[h, keys, :] += jnp.dot(
                    score_grad, q_rows[h, cols, :], preferred_element_type=F32
                )
                dq_ref[rows, cols] += jnp.dot(
                    kv_ref[rows, keys], score_grad, preferred_element_type=F32
                )
            return 0

        lax.fori_loop(lo_ref[b], hi_ref[b], key_block, 0)
        dq_ref[:, cols] = dq_ref[:, cols] * scale
        return 0

    lax.fori_loop(0, tokens // bq, query_block, 0)

    def finish(step, _):
        at = pl.multiple_of(step * bk, bk)
        for h in range(heads):
            rows = slice(h * head_dim, (h + 1) * head_dim)
            low = slice(width + h * head_dim, width + (h + 1) * head_dim)
            dkv_ref[rows, pl.ds(at, bk)] = dk_acc[h, pl.ds(at, bk), :].T.astype(dkv_ref.dtype)
            dkv_ref[low, pl.ds(at, bk)] = dv_acc[h, pl.ds(at, bk), :].T.astype(dkv_ref.dtype)
        return 0

    lax.fori_loop(0, tokens // bk, finish, 0)


def vmem(count):
    return [pl.BlockSpec(memory_space=pltpu.VMEM)] * count


def attention_forward(heads, head_dim, lo, hi, start, q, kv0, kv1, do):
    tokens = q.shape[1]
    bq, bk = block_sizes(tokens)
    width = heads * head_dim
    return pl.pallas_call(
        functools.partial(forward_kernel, heads, head_dim, bq, bk),
        out_shape=(
            jax.ShapeDtypeStruct((width, tokens), BF16),
            jax.ShapeDtypeStruct((heads, 1, tokens), F32),
            jax.ShapeDtypeStruct((heads, 1, tokens), F32),
        ),
        in_specs=[pl.BlockSpec(memory_space=pltpu.SMEM)] * 2 + vmem(5),
        out_specs=tuple(vmem(3)),
        scratch_shapes=[
            pltpu.VMEM((heads, 2 * tokens, head_dim), BF16),
            pltpu.VMEM((width, 2 * tokens), BF16),
            pltpu.VMEM((heads, head_dim, bq), F32),
            pltpu.VMEM((heads, 1, bq), F32),
            pltpu.VMEM((heads, 1, bq), F32),
        ],
        compiler_params=pltpu.CompilerParams(vmem_limit_bytes=VMEM_BYTES),
        cost_estimate=pl.CostEstimate(
            flops=0, bytes_accessed=8 * width * tokens * 2, transcendentals=0
        ),
        name="attention_forward",
    )(lo, hi, start, q, kv0, kv1, do)


def attention_backward(heads, head_dim, q_off, kind, lo, hi, start, q, do, lse, dot, kv):
    tokens = q.shape[1]
    bq, bk = block_sizes(tokens)
    width = heads * head_dim
    return pl.pallas_call(
        functools.partial(backward_kernel, heads, head_dim, bq, bk, q_off),
        out_shape=(
            jax.ShapeDtypeStruct((width, tokens), F32),
            jax.ShapeDtypeStruct((2 * width, tokens), kind),
        ),
        in_specs=[pl.BlockSpec(memory_space=pltpu.SMEM)] * 2 + vmem(6),
        out_specs=tuple(vmem(2)),
        scratch_shapes=[pltpu.VMEM((heads, tokens, head_dim), BF16)] * 4
        + [pltpu.VMEM((heads, tokens, head_dim), F32)] * 2,
        compiler_params=pltpu.CompilerParams(vmem_limit_bytes=VMEM_BYTES),
        cost_estimate=pl.CostEstimate(
            flops=0, bytes_accessed=8 * width * tokens * 2, transcendentals=0
        ),
        name="attention_cross_back" if q_off else "attention_own_back",
    )(lo, hi, start, q, do, lse, dot, kv)


def project_kernel(
    heads,
    head_dim,
    bn,
    x_ref,
    w_ref,
    bias_ref,
    norm_ref,
    cos_ref,
    sin_ref,
    q_ref,
    kv_ref,
    attn_ref,
    mlp_ref,
    w_cols,
):
    width = heads * head_dim
    half = head_dim // 8
    w_cols[...] = w_ref[...].astype(F32).T.astype(BF16)

    def one(step, _):
        cols = pl.ds(pl.multiple_of(step * bn, bn), bn)
        x = x_ref[cols, :].astype(F32)
        centred = x - jnp.mean(x, axis=-1, keepdims=True)
        unit = centred * lax.rsqrt(jnp.mean(centred * centred, axis=-1, keepdims=True) + 1e-05)
        normed = (unit * norm_ref[0:1, :] + norm_ref[2:3, :]).astype(BF16)
        attn_ref[cols, :] = normed
        mlp_ref[cols, :] = (unit * norm_ref[1:2, :] + norm_ref[3:4, :]).astype(BF16)
        projected = (
            lax.dot_general(
                w_cols[...], normed, (((1,), (1,)), ((), ())), preferred_element_type=F32
            )
            + bias_ref[...]
        )
        cosine, sine_wave = cos_ref[:, cols], sin_ref[:, cols]
        for i in range(2):
            target = kv_ref if i else q_ref
            scale = 1.0 if i else head_dim**-0.5
            for h in range(heads):
                at, to = i * width + h * head_dim, h * head_dim
                first = projected[at : at + half]
                second = projected[at + half : at + 2 * half]
                turned = jnp.concatenate(
                    [
                        first * cosine - second * sine_wave,
                        second * cosine + first * sine_wave,
                        projected[at + 2 * half : at + head_dim],
                    ],
                    axis=0,
                )
                target[to : to + head_dim, cols] = (turned * scale).astype(BF16)
        kv_ref[width:, cols] = projected[2 * width :].astype(BF16)
        return 0

    lax.fori_loop(0, x_ref.shape[0] // bn, one, 0)


def project(heads, head_dim, x, w, bias, norms, cosine, sine_wave):
    tokens, model = x.shape
    width = heads * head_dim
    return pl.pallas_call(
        functools.partial(project_kernel, heads, head_dim, min(512, tokens)),
        out_shape=(
            jax.ShapeDtypeStruct((width, tokens), BF16),
            jax.ShapeDtypeStruct((2 * width, tokens), BF16),
            jax.ShapeDtypeStruct((tokens, model), BF16),
            jax.ShapeDtypeStruct((tokens, model), BF16),
        ),
        in_specs=vmem(6),
        out_specs=tuple(vmem(4)),
        scratch_shapes=[pltpu.VMEM((3 * width, model), BF16)],
        compiler_params=pltpu.CompilerParams(vmem_limit_bytes=VMEM_BYTES),
        cost_estimate=pl.CostEstimate(
            flops=0, bytes_accessed=6 * tokens * model, transcendentals=0
        ),
        name="project",
    )(x, w, bias, norms, cosine, sine_wave)


def rotate(field, cosine, sine_wave, direction, heads, head_dim):
    shaped = field.reshape(heads, head_dim, field.shape[1])
    half = head_dim // 8
    first, second = shaped[:, :half], shaped[:, half : 2 * half]
    turned = jnp.concatenate(
        [
            first * cosine - direction * second * sine_wave,
            second * cosine + direction * first * sine_wave,
            shaped[:, 2 * half :],
        ],
        axis=1,
    )
    return turned.reshape(field.shape)


def axis_swap(value, axis, bit):
    size = lax.axis_size(axis)
    return lax.ppermute(value, axis, [(i, i ^ bit) for i in range(size)])


def sum_pairs(value, axis):
    size = lax.axis_size(axis)
    if size & (size - 1):
        return lax.psum(value, axis)
    bit = 1
    while bit < size:
        value = value + axis_swap(value, axis, bit)
        bit *= 2
    return value


def gather_rows(part, after=()):
    peers = lax.axis_size("fsdp")
    if peers > 4:
        return lax.all_gather(part, "fsdp", axis=0, tiled=True)
    me, rows = lax.axis_index("fsdp"), part.shape[0]
    whole = jnp.zeros((peers * rows, part.shape[1]), part.dtype)
    for by in range(peers):
        if by == 0:
            piece, _ = lax.optimization_barrier((part, after))
        else:
            piece = lax.ppermute(part, "fsdp", [(i, (i + by) % peers) for i in range(peers)])
        whole = lax.dynamic_update_slice_in_dim(whole, piece, ((me - by) % peers) * rows, 0)
    return whole


def gather_small(part):
    peers = lax.axis_size("fsdp")
    if peers > 4:
        return lax.all_gather(part, "fsdp")
    pieces = [part] + [
        lax.ppermute(part, "fsdp", [(i, (i + by) % peers) for i in range(peers)])
        for by in range(1, peers)
    ]
    ring = jnp.stack([pieces[-step % peers] for step in range(2 * peers)])
    first = -lax.axis_index("fsdp") % peers
    return lax.dynamic_slice_in_dim(ring, first, peers, 0)


def scatter_rows(part, after=()):
    peers = lax.axis_size("fsdp")
    if peers > 4:
        total = lax.psum_scatter(part, "fsdp", scatter_dimension=0, tiled=True).astype(F32)
    else:
        me, rows = lax.axis_index("fsdp"), part.shape[0] // peers
        own, _ = lax.optimization_barrier(
            (lax.dynamic_slice_in_dim(part, me * rows, rows, 0), after)
        )
        total = own.astype(F32)
        for by in range(1, peers):
            send = lax.dynamic_slice_in_dim(part, ((me + by) % peers) * rows, rows, 0)
            got = lax.ppermute(send, "fsdp", [(i, (i + by) % peers) for i in range(peers)])
            total = total + got.astype(F32)
    return lax.optimization_barrier(total.astype(BF16))


def ctx_sum(low):
    if lax.axis_size("ctx") != 2:
        return lax.psum(low, "ctx").astype(F32)
    return low.astype(F32) + axis_swap(low, "ctx", 1).astype(F32)


def tp_half(whole):
    core = lax.axis_index("tp") % 2
    rows = whole.shape[0] // 2
    return (
        lax.dynamic_slice_in_dim(whole, core * rows, rows, 0),
        lax.dynamic_slice_in_dim(whole, (1 - core) * rows, rows, 0),
    )


def tp_sum_core(part):
    mine, other = tp_half(part)
    half = mine.astype(F32) + axis_swap(other, "tp", 1).astype(F32)
    return lax.optimization_barrier(half.astype(BF16))


def tp_sum_chips(low, after=()):
    own, _ = lax.optimization_barrier((low, after))
    half = own.astype(F32)
    bit = 2
    while bit < lax.axis_size("tp"):
        if bit > 2:
            low = lax.optimization_barrier(half.astype(BF16))
            half = low.astype(F32)
        half = half + axis_swap(low, "tp", bit).astype(F32)
        bit *= 2
    return half


def tp_join(half):
    half = lax.optimization_barrier(half)
    other = axis_swap(half, "tp", 1)
    first = lax.axis_index("tp") % 2 == 0
    return [jnp.where(first, half, other), jnp.where(first, other, half)]


def on_device(
    hidden_in,
    segments,
    positions,
    norm_gains,
    norm_biases,
    qkv_weight,
    qkv_bias,
    out_weight,
    up_weight,
    up_bias,
    down_weight,
    branch_biases,
    out_grad,
):
    rows, tokens, model = hidden_in.shape
    assert rows == 1
    fsdp = lax.axis_size("fsdp")
    ctx_size = lax.axis_size("ctx")
    tp = lax.axis_size("tp")
    ctx_index = lax.axis_index("ctx")
    heads, head_dim = qkv_bias.shape[1], qkv_bias.shape[2] * fsdp
    width = heads * head_dim
    hidden_units = up_weight.shape[1]
    shard_rows = qkv_weight.shape[1]
    barrier = lax.optimization_barrier

    segs = segments.reshape(tokens)
    shift = [(i, i + 1) for i in range(ctx_size - 1)]
    back = [(i + 1, i) for i in range(ctx_size - 1)]
    w_qkv = gather_rows(jnp.transpose(qkv_weight, (1, 0, 2)).reshape(shard_rows, 3 * width))
    norms = jnp.concatenate([norm_gains, norm_biases, branch_biases], axis=0)
    biases = jnp.concatenate([qkv_bias.reshape(3 * heads, -1), up_bias], axis=0)
    bias_rows, bias_cols = biases.shape
    pack = jnp.concatenate(
        [norms, jnp.pad(biases, ((0, 0), (0, shard_rows - bias_cols)))], axis=0
    )
    pack = gather_small(jnp.pad(pack, ((0, -pack.shape[0] % 16), (0, 0)))).astype(F32)
    norms = jnp.transpose(pack[:, :6], (1, 0, 2)).reshape(6, model)
    gains, branch_bias = norms[0:2], norms[4:6]
    biases = jnp.transpose(pack[:, 6 : 6 + bias_rows, :bias_cols], (1, 0, 2)).reshape(-1)
    b_qkv, b_up = biases[: 3 * width], biases[3 * width :]
    second = jnp.concatenate([up_weight, out_weight.T], axis=1)
    w_qkv, second, segs = barrier((w_qkv, second, segs))
    earlier_segs = lax.ppermute(segs, "ctx", shift)
    second = gather_rows(second)
    third, second = barrier((down_weight.T, second))
    w_up, w_out = second[:, :hidden_units], second[:, hidden_units:]

    earlier_segs = jnp.where(ctx_index == 0, -1, earlier_segs)
    segs_all = jnp.concatenate([earlier_segs, segs])
    start = jnp.sum((segs_all[:, None] < segs[None, :]).astype(jnp.int32), axis=0)
    bq, bk = block_sizes(tokens)
    blocks = tokens // bq
    start_block = start.reshape(blocks, bq)[:, 0]
    ends = (jnp.arange(blocks, dtype=jnp.int32) + 1) * bq
    own_hi = (ends + bk - 1) // bk
    fwd_lo, fwd_hi = start_block // bk, own_hi + tokens // bk
    own_lo = jnp.maximum(start_block - tokens, 0) // bk
    cross_hi = jnp.full((blocks,), tokens // bk, jnp.int32)
    cross_lo = jnp.minimum(start_block // bk, cross_hi)
    start_row = start.reshape(1, tokens)

    residual = hidden_in.reshape(tokens, model).astype(F32)
    centred = residual - jnp.mean(residual, axis=-1, keepdims=True)
    inv_spread = lax.rsqrt(jnp.mean(centred * centred, axis=-1, keepdims=True) + 1e-05)
    normal_unit = centred * inv_spread
    rot_width = head_dim // 4
    frequency = jnp.power(10000.0, -jnp.arange(0, rot_width, 2).astype(F32) / rot_width)
    angles = positions.reshape(1, tokens).astype(F32) * frequency[:, None]
    cosine, sine_wave = jnp.cos(angles), jnp.sin(angles)
    q, kv, normed_attn, normed_mlp = project(
        heads,
        head_dim,
        hidden_in.reshape(tokens, model),
        w_qkv,
        b_qkv[:, None],
        norms,
        cosine,
        sine_wave,
    )
    kv0 = lax.ppermute(kv, "ctx", shift)

    grad_low = out_grad.reshape(tokens, model)
    up_pre = jnp.dot(normed_mlp, w_up, preferred_element_type=F32) + b_up
    cdf = 0.5 * (1.0 + lax.erf(up_pre * math.sqrt(0.5)))
    activated = (up_pre * cdf).astype(BF16)
    slope = (cdf + up_pre * (jnp.exp(-0.5 * up_pre * up_pre) * (1 / math.sqrt(2 * math.pi)))).astype(
        BF16
    )
    do = jnp.einsum("nd,de->en", grad_low, w_out, preferred_element_type=F32).astype(BF16)
    activated, slope, do = barrier((activated, slope, do))
    down_part = jnp.einsum("nd,nf->df", grad_low, activated, preferred_element_type=F32)
    w_down = gather_rows(third)
    down_part, do, w_down = barrier((down_part.astype(BF16), do, w_down))
    mixed, lse, dot = attention_forward(
        heads, head_dim, fwd_lo, fwd_hi, start_row, q, kv0, kv, do
    )

    down_sum = scatter_rows(down_part, mixed)
    down_sum, lse = barrier((down_sum, lse))
    dq0, dkv0 = attention_backward(
        heads, head_dim, tokens, BF16, cross_lo, cross_hi, start_row, q, do, lse, dot, kv0
    )
    dkv_back = lax.ppermute(dkv0, "ctx", back)

    activated, slope, dq0 = barrier((activated, slope, dq0))
    branch_part = jnp.einsum("en,de->nd", mixed, w_out, preferred_element_type=F32) + jnp.einsum(
        "nf,df->nd", activated, w_down, preferred_element_type=F32
    )
    branch_part, slope = barrier((branch_part.astype(BF16), slope))
    act_grad = jnp.einsum("nd,df->nf", grad_low, w_down, preferred_element_type=F32)
    up_grad = barrier((act_grad * slope.astype(F32)).astype(BF16))
    up_part = jnp.einsum("nd,nf->df", normed_mlp, up_grad, preferred_element_type=F32)
    up_part = up_part.astype(BF16)
    branch_low = tp_sum_core(branch_part)
    up_part, branch_low, lse = barrier((up_part, branch_low, lse))
    dq1, dkv1 = attention_backward(
        heads, head_dim, 0, F32, own_lo, own_hi, start_row - tokens, q, do, lse, dot, kv
    )
    branch_half = tp_sum_chips(branch_low, dq1)
    up_grad, mixed, dq1, branch_half = barrier((up_grad, mixed, dq1, branch_half))
    mlp_norm_grad = jnp.einsum("nf,df->nd", up_grad, w_up, preferred_element_type=F32)
    up_bias_part = jnp.sum(up_grad, axis=0, dtype=F32)
    branch_row = jnp.sum(grad_low, axis=0, dtype=F32)
    out_part = jnp.einsum("nd,en->de", grad_low, mixed, preferred_element_type=F32).astype(BF16)
    up_sum = scatter_rows(up_part, (mlp_norm_grad, out_part))
    dkv_back, up_sum, dkv1, dq1, mlp_norm_grad = barrier(
        (dkv_back, up_sum, dkv1, dq1, mlp_norm_grad)
    )
    mlp_sum = jnp.concatenate([up_sum, down_sum], axis=1)
    residual_half, _ = tp_half(hidden_in.reshape(tokens, model))
    hidden_half = (
        residual_half.astype(F32) + branch_half + branch_bias[0] + branch_bias[1]
    ).astype(BF16)

    dkv = dkv1 + dkv_back.astype(F32)
    projected_grad = jnp.concatenate(
        [
            rotate(dq0 + dq1, cosine, sine_wave, -1.0, heads, head_dim),
            rotate(dkv[:width], cosine, sine_wave, -1.0, heads, head_dim),
            dkv[width:],
        ],
        axis=0,
    ).astype(BF16)
    projected_grad = barrier(projected_grad)

    attn_norm_grad = jnp.einsum("en,de->nd", projected_grad, w_qkv, preferred_element_type=F32)
    unit_part = attn_norm_grad * gains[0] + mlp_norm_grad * gains[1]
    unit_low = tp_sum_core(barrier(unit_part.astype(BF16)))
    qkv_part = jnp.einsum("nd,en->de", normed_attn, projected_grad, preferred_element_type=F32)
    last_part = jnp.concatenate([qkv_part.astype(BF16), out_part], axis=1)
    qkv_bias_part = jnp.sum(projected_grad, axis=1, dtype=F32)

    tp_index = lax.axis_index("tp")
    everywhere = jnp.concatenate(
        [
            jnp.sum(attn_norm_grad * normal_unit, axis=0),
            jnp.sum(mlp_norm_grad * normal_unit, axis=0),
            jnp.sum(attn_norm_grad, axis=0),
            jnp.sum(mlp_norm_grad, axis=0),
            jnp.where(tp_index == 0, branch_row, 0.0),
        ]
    )
    own = jnp.concatenate([qkv_bias_part, up_bias_part])
    slots = jnp.where(jnp.arange(tp)[:, None] == tp_index, own[None], 0.0)
    sums = jnp.concatenate([everywhere, slots.reshape(-1)])
    unit_low, last_part, sums, mlp_sum, hidden_half, hidden_tail = barrier(
        (unit_low, last_part, sums, mlp_sum, hidden_half, hidden_in.reshape(tokens, model))
    )
    unit_grad = tp_sum_chips(unit_low)
    last_sum = scatter_rows(last_part)
    last_sum, sums = barrier((last_sum, sums))
    mlp_grad = ctx_sum(mlp_sum)
    for axis in ("tp", "ctx", "fsdp"):
        sums = sum_pairs(sums, axis)
    hidden_out = jnp.concatenate(tp_join(hidden_half), axis=0)
    hidden_tail, _ = tp_half(hidden_tail)
    residual_tail = hidden_tail.astype(F32)
    centred_tail = residual_tail - jnp.mean(residual_tail, axis=-1, keepdims=True)
    spread_tail = lax.rsqrt(jnp.mean(centred_tail * centred_tail, axis=-1, keepdims=True) + 1e-05)
    unit = centred_tail * spread_tail
    grad_tail, _ = tp_half(grad_low)
    input_half = grad_tail.astype(F32) + spread_tail * (
        unit_grad
        - jnp.mean(unit_grad, axis=-1, keepdims=True)
        - unit * jnp.mean(unit_grad * unit, axis=-1, keepdims=True)
    )
    input_grad = jnp.concatenate(tp_join(input_half.astype(BF16)), axis=0)
    last_grad = ctx_sum(last_sum)
    qkv_weight_grad = jnp.transpose(
        last_grad[:, : 3 * width].reshape(shard_rows, 3, width), (1, 0, 2)
    )
    out_weight_grad = last_grad[:, 3 * width :].T
    up_weight_grad = mlp_grad[:, :hidden_units]
    down_weight_grad = mlp_grad[:, hidden_units:].T
    norm_sums = sums[: 5 * model].reshape(5, model)
    own_sums = lax.dynamic_index_in_dim(
        sums[5 * model :].reshape(tp, -1), tp_index, axis=0, keepdims=False
    )
    fsdp_index = lax.axis_index("fsdp")

    def shard(whole):
        size = whole.shape[-1] // fsdp
        return lax.dynamic_slice_in_dim(whole, fsdp_index * size, size, axis=whole.ndim - 1)

    norm_sums = shard(norm_sums)
    qkv_bias_grad = shard(own_sums[: 3 * width].reshape(3, heads, head_dim))
    up_bias_grad = shard(own_sums[3 * width :].reshape(-1, head_dim))
    return (
        hidden_out.reshape(hidden_in.shape),
        input_grad.reshape(hidden_in.shape),
        norm_sums[0:2],
        norm_sums[2:4],
        qkv_weight_grad,
        qkv_bias_grad,
        out_weight_grad,
        up_weight_grad,
        up_bias_grad,
        down_weight_grad,
        jnp.stack([norm_sums[4], norm_sums[4]]),
    )


def solution(mesh):
    return jax.shard_map(
        on_device,
        mesh=mesh,
        in_specs=(
            P("fsdp", "ctx", None),
            P("fsdp", "ctx"),
            P("fsdp", "ctx"),
            P(None, "fsdp"),
            P(None, "fsdp"),
            P(None, "fsdp", "tp"),
            P(None, "tp", "fsdp"),
            P("tp", "fsdp"),
            P("fsdp", "tp"),
            P("tp", "fsdp"),
            P("tp", "fsdp"),
            P(None, "fsdp"),
            P("fsdp", "ctx", None),
        ),
        out_specs=(
            P("fsdp", "ctx", None),
            P("fsdp", "ctx", None),
            P(None, "fsdp"),
            P(None, "fsdp"),
            P(None, "fsdp", "tp"),
            P(None, "tp", "fsdp"),
            P("tp", "fsdp"),
            P("fsdp", "tp"),
            P("tp", "fsdp"),
            P("tp", "fsdp"),
            P(None, "fsdp"),
        ),
        check_vma=False,
    )
```

```python
import functools
import math

import jax
import jax.numpy as jnp
from jax import lax
from jax.experimental import pallas as pl
from jax.experimental.pallas import tpu as pltpu
from jax.sharding import PartitionSpec as P

F32 = jnp.float32
BF16 = jnp.bfloat16
VMEM_BYTES = 56 * 1024 * 1024


def block_sizes(tokens):
    return min(256, tokens), min(256, tokens)


def to_rows(source, first, target, heads, head_dim, chunk):
    def one(step, _):
        at = pl.multiple_of(step * chunk, chunk)
        for h in range(heads):
            part = source[first + h * head_dim : first + (h + 1) * head_dim, pl.ds(at, chunk)]
            target[h, pl.ds(at, chunk), :] = part.astype(F32).T.astype(BF16)
        return 0

    lax.fori_loop(0, source.shape[1] // chunk, one, 0)


def allowed_keys(start_row, at_key, at_query, q_off, bk, bq):
    key = lax.broadcasted_iota(jnp.int32, (bk, bq), 0)
    query = lax.broadcasted_iota(jnp.int32, (1, bq), 1) + (at_query + q_off - at_key)
    return (key >= start_row - at_key) & (key <= query)


def forward_kernel(
    heads,
    head_dim,
    bq,
    bk,
    lo_ref,
    hi_ref,
    start_ref,
    q_ref,
    kv0_ref,
    kv1_ref,
    do_ref,
    out_ref,
    lse_ref,
    dot_ref,
    k_rows,
    v_cols,
    acc,
    top,
    total,
):
    tokens = q_ref.shape[1]
    width = heads * head_dim

    def fill(source, offset):
        def one(step, _):
            at = pl.multiple_of(step * bk, bk)
            to = pl.multiple_of(step * bk + offset, bk)
            for h in range(heads):
                part = source[h * head_dim : (h + 1) * head_dim, pl.ds(at, bk)]
                k_rows[h, pl.ds(to, bk), :] = part.astype(F32).T.astype(BF16)
            return 0

        lax.fori_loop(0, tokens // bk, one, 0)

    fill(kv0_ref, 0)
    fill(kv1_ref, tokens)
    v_cols[:, :tokens] = kv0_ref[width:, :]
    v_cols[:, tokens:] = kv1_ref[width:, :]

    def query_block(b, _):
        at_query = pl.multiple_of(b * bq, bq)
        cols = pl.ds(at_query, bq)
        start_row = start_ref[:, cols]
        acc[...] = jnp.zeros_like(acc)
        top[...] = jnp.full_like(top, -1e30)
        total[...] = jnp.zeros_like(total)

        def key_block(kb, _):
            at_key = pl.multiple_of(kb * bk, bk)
            allowed = allowed_keys(start_row, at_key, at_query, tokens, bk, bq)
            for h in range(heads):
                rows = slice(h * head_dim, (h + 1) * head_dim)
                scores = jnp.dot(
                    k_rows[h, pl.ds(at_key, bk), :],
                    q_ref[rows, cols],
                    preferred_element_type=F32,
                )
                scores = jnp.where(allowed, scores, -1e30)
                old = top[h]
                new = jnp.maximum(old, jnp.max(scores, axis=0, keepdims=True))
                weights = jnp.exp(scores - new)
                shrink = jnp.exp(old - new)
                top[h] = new
                total[h] = total[h] * shrink + jnp.sum(weights, axis=0, keepdims=True)
                acc[h] = acc[h] * shrink + jnp.dot(
                    v_cols[rows, pl.ds(at_key, bk)],
                    weights.astype(BF16),
                    preferred_element_type=F32,
                )
            return 0

        lax.fori_loop(lo_ref[b], hi_ref[b], key_block, 0)
        for h in range(heads):
            rows = slice(h * head_dim, (h + 1) * head_dim)
            mixed = acc[h] / total[h]
            out_ref[rows, cols] = mixed.astype(BF16)
            lse_ref[h, :, cols] = top[h] + jnp.log(total[h])
            dot_ref[h, :, cols] = jnp.sum(
                mixed * do_ref[rows, cols].astype(F32), axis=0, keepdims=True
            )
        return 0

    lax.fori_loop(0, tokens // bq, query_block, 0)


def backward_kernel(
    heads,
    head_dim,
    bq,
    bk,
    q_off,
    lo_ref,
    hi_ref,
    start_ref,
    q_ref,
    do_ref,
    lse_ref,
    dot_ref,
    kv_ref,
    dq_ref,
    dkv_ref,
    q_rows,
    do_rows,
    k_rows,
    v_rows,
    dk_acc,
    dv_acc,
):
    tokens = q_ref.shape[1]
    width = heads * head_dim
    scale = head_dim**-0.5
    for source, first, target in (
        (q_ref, 0, q_rows),
        (do_ref, 0, do_rows),
        (kv_ref, 0, k_rows),
        (kv_ref, width, v_rows),
    ):
        to_rows(source, first, target, heads, head_dim, bk)
    dk_acc[...] = jnp.zeros_like(dk_acc)
    dv_acc[...] = jnp.zeros_like(dv_acc)
    dq_ref[...] = jnp.zeros_like(dq_ref)

    def query_block(b, _):
        at_query = pl.multiple_of(b * bq, bq)
        cols = pl.ds(at_query, bq)
        start_row = start_ref[:, cols]

        def key_block(kb, _):
            at_key = pl.multiple_of(kb * bk, bk)
            keys = pl.ds(at_key, bk)
            allowed = allowed_keys(start_row, at_key, at_query, q_off, bk, bq)
            for h in range(heads):
                rows = slice(h * head_dim, (h + 1) * head_dim)
                scores = jnp.dot(
                    k_rows[h, keys, :], q_ref[rows, cols], preferred_element_type=F32
                )
                prob = jnp.exp(jnp.where(allowed, scores - lse_ref[h, :, cols], -1e30))
                prob_grad = jnp.dot(
                    v_rows[h, keys, :], do_ref[rows, cols], preferred_element_type=F32
                )
                score_grad = (prob * (prob_grad - dot_ref[h, :, cols])).astype(BF16)
                dv_acc[h, keys, :] += jnp.dot(
                    prob.astype(BF16), do_rows[h, cols, :], preferred_element_type=F32
                )
                dk_acc[h, keys, :] += jnp.dot(
                    score_grad, q_rows[h, cols, :], preferred_element_type=F32
                )
                dq_ref[rows, cols] += jnp.dot(
                    kv_ref[rows, keys], score_grad, preferred_element_type=F32
                )
            return 0

        lax.fori_loop(lo_ref[b], hi_ref[b], key_block, 0)
        dq_ref[:, cols] = dq_ref[:, cols] * scale
        return 0

    lax.fori_loop(0, tokens // bq, query_block, 0)

    def finish(step, _):
        at = pl.multiple_of(step * bk, bk)
        for h in range(heads):
            rows = slice(h * head_dim, (h + 1) * head_dim)
            low = slice(width + h * head_dim, width + (h + 1) * head_dim)
            dkv_ref[rows, pl.ds(at, bk)] = dk_acc[h, pl.ds(at, bk), :].T.astype(dkv_ref.dtype)
            dkv_ref[low, pl.ds(at, bk)] = dv_acc[h, pl.ds(at, bk), :].T.astype(dkv_ref.dtype)
        return 0

    lax.fori_loop(0, tokens // bk, finish, 0)


def vmem(count):
    return [pl.BlockSpec(memory_space=pltpu.VMEM)] * count


def attention_forward(heads, head_dim, lo, hi, start, q, kv0, kv1, do):
    tokens = q.shape[1]
    bq, bk = block_sizes(tokens)
    width = heads * head_dim
    return pl.pallas_call(
        functools.partial(forward_kernel, heads, head_dim, bq, bk),
        out_shape=(
            jax.ShapeDtypeStruct((width, tokens), BF16),
            jax.ShapeDtypeStruct((heads, 1, tokens), F32),
            jax.ShapeDtypeStruct((heads, 1, tokens), F32),
        ),
        in_specs=[pl.BlockSpec(memory_space=pltpu.SMEM)] * 2 + vmem(5),
        out_specs=tuple(vmem(3)),
        scratch_shapes=[
            pltpu.VMEM((heads, 2 * tokens, head_dim), BF16),
            pltpu.VMEM((width, 2 * tokens), BF16),
            pltpu.VMEM((heads, head_dim, bq), F32),
            pltpu.VMEM((heads, 1, bq), F32),
            pltpu.VMEM((heads, 1, bq), F32),
        ],
        compiler_params=pltpu.CompilerParams(vmem_limit_bytes=VMEM_BYTES),
        cost_estimate=pl.CostEstimate(
            flops=0, bytes_accessed=8 * width * tokens * 2, transcendentals=0
        ),
        name="attention_forward",
    )(lo, hi, start, q, kv0, kv1, do)


def attention_backward(heads, head_dim, q_off, kind, lo, hi, start, q, do, lse, dot, kv):
    tokens = q.shape[1]
    bq, bk = block_sizes(tokens)
    width = heads * head_dim
    return pl.pallas_call(
        functools.partial(backward_kernel, heads, head_dim, bq, bk, q_off),
        out_shape=(
            jax.ShapeDtypeStruct((width, tokens), F32),
            jax.ShapeDtypeStruct((2 * width, tokens), kind),
        ),
        in_specs=[pl.BlockSpec(memory_space=pltpu.SMEM)] * 2 + vmem(6),
        out_specs=tuple(vmem(2)),
        scratch_shapes=[pltpu.VMEM((heads, tokens, head_dim), BF16)] * 4
        + [pltpu.VMEM((heads, tokens, head_dim), F32)] * 2,
        compiler_params=pltpu.CompilerParams(vmem_limit_bytes=VMEM_BYTES),
        cost_estimate=pl.CostEstimate(
            flops=0, bytes_accessed=8 * width * tokens * 2, transcendentals=0
        ),
        name="attention_cross_back" if q_off else "attention_own_back",
    )(lo, hi, start, q, do, lse, dot, kv)


def project_kernel(
    heads,
    head_dim,
    bn,
    x_ref,
    w_ref,
    bias_ref,
    norm_ref,
    cos_ref,
    sin_ref,
    q_ref,
    kv_ref,
    attn_ref,
    mlp_ref,
    unit_ref,
    w_cols,
):
    width = heads * head_dim
    half = head_dim // 8
    w_cols[...] = w_ref[...].astype(F32).T.astype(BF16)

    def one(step, _):
        cols = pl.ds(pl.multiple_of(step * bn, bn), bn)
        x = x_ref[cols, :].astype(F32)
        centred = x - jnp.mean(x, axis=-1, keepdims=True)
        unit = centred * lax.rsqrt(jnp.mean(centred * centred, axis=-1, keepdims=True) + 1e-05)
        normed = (unit * norm_ref[0:1, :] + norm_ref[2:3, :]).astype(BF16)
        attn_ref[cols, :] = normed
        unit_ref[cols, :] = unit.astype(BF16)
        mlp_ref[cols, :] = (unit * norm_ref[1:2, :] + norm_ref[3:4, :]).astype(BF16)
        projected = (
            lax.dot_general(
                w_cols[...], normed, (((1,), (1,)), ((), ())), preferred_element_type=F32
            )
            + bias_ref[...]
        )
        cosine, sine_wave = cos_ref[:, cols], sin_ref[:, cols]
        for i in range(2):
            target = kv_ref if i else q_ref
            scale = 1.0 if i else head_dim**-0.5
            for h in range(heads):
                at, to = i * width + h * head_dim, h * head_dim
                first = projected[at : at + half]
                second = projected[at + half : at + 2 * half]
                turned = jnp.concatenate(
                    [
                        first * cosine - second * sine_wave,
                        second * cosine + first * sine_wave,
                        projected[at + 2 * half : at + head_dim],
                    ],
                    axis=0,
                )
                target[to : to + head_dim, cols] = (turned * scale).astype(BF16)
        kv_ref[width:, cols] = projected[2 * width :].astype(BF16)
        return 0

    lax.fori_loop(0, x_ref.shape[0] // bn, one, 0)


def project(heads, head_dim, x, w, bias, norms, cosine, sine_wave):
    tokens, model = x.shape
    width = heads * head_dim
    return pl.pallas_call(
        functools.partial(project_kernel, heads, head_dim, min(512, tokens)),
        out_shape=(
            jax.ShapeDtypeStruct((width, tokens), BF16),
            jax.ShapeDtypeStruct((2 * width, tokens), BF16),
            jax.ShapeDtypeStruct((tokens, model), BF16),
            jax.ShapeDtypeStruct((tokens, model), BF16),
            jax.ShapeDtypeStruct((tokens, model), BF16),
        ),
        in_specs=vmem(6),
        out_specs=tuple(vmem(5)),
        scratch_shapes=[pltpu.VMEM((3 * width, model), BF16)],
        compiler_params=pltpu.CompilerParams(vmem_limit_bytes=VMEM_BYTES),
        cost_estimate=pl.CostEstimate(
            flops=0, bytes_accessed=6 * tokens * model, transcendentals=0
        ),
        name="project",
    )(x, w, bias, norms, cosine, sine_wave)


def rotate(field, cosine, sine_wave, direction, heads, head_dim):
    shaped = field.reshape(heads, head_dim, field.shape[1])
    half = head_dim // 8
    first, second = shaped[:, :half], shaped[:, half : 2 * half]
    turned = jnp.concatenate(
        [
            first * cosine - direction * second * sine_wave,
            second * cosine + direction * first * sine_wave,
            shaped[:, 2 * half :],
        ],
        axis=1,
    )
    return turned.reshape(field.shape)


def axis_swap(value, axis, bit):
    size = lax.axis_size(axis)
    return lax.ppermute(value, axis, [(i, i ^ bit) for i in range(size)])


def sum_pairs(value, axis):
    size = lax.axis_size(axis)
    if size & (size - 1):
        return lax.psum(value, axis)
    bit = 1
    while bit < size:
        value = value + axis_swap(value, axis, bit)
        bit *= 2
    return value


def gather_rows(part, after=()):
    peers = lax.axis_size("fsdp")
    if peers > 4:
        return lax.all_gather(part, "fsdp", axis=0, tiled=True)
    me, rows = lax.axis_index("fsdp"), part.shape[0]
    whole = jnp.zeros((peers * rows, part.shape[1]), part.dtype)
    for by in range(peers):
        if by == 0:
            piece, _ = lax.optimization_barrier((part, after))
        else:
            piece = lax.ppermute(part, "fsdp", [(i, (i + by) % peers) for i in range(peers)])
        whole = lax.dynamic_update_slice_in_dim(whole, piece, ((me - by) % peers) * rows, 0)
    return whole


def gather_small(part):
    peers = lax.axis_size("fsdp")
    if peers > 4:
        return lax.all_gather(part, "fsdp")
    pieces = [part] + [
        lax.ppermute(part, "fsdp", [(i, (i + by) % peers) for i in range(peers)])
        for by in range(1, peers)
    ]
    ring = jnp.stack([pieces[-step % peers] for step in range(2 * peers)])
    first = -lax.axis_index("fsdp") % peers
    return lax.dynamic_slice_in_dim(ring, first, peers, 0)


def scatter_rows(part, after=()):
    peers = lax.axis_size("fsdp")
    if peers > 4:
        total = lax.psum_scatter(part, "fsdp", scatter_dimension=0, tiled=True).astype(F32)
    else:
        me, rows = lax.axis_index("fsdp"), part.shape[0] // peers
        own, _ = lax.optimization_barrier(
            (lax.dynamic_slice_in_dim(part, me * rows, rows, 0), after)
        )
        total = own.astype(F32)
        for by in range(1, peers):
            send = lax.dynamic_slice_in_dim(part, ((me + by) % peers) * rows, rows, 0)
            got = lax.ppermute(send, "fsdp", [(i, (i + by) % peers) for i in range(peers)])
            total = total + got.astype(F32)
    return lax.optimization_barrier(total.astype(BF16))


def ctx_sum(low):
    if lax.axis_size("ctx") != 2:
        return lax.psum(low, "ctx").astype(F32)
    return low.astype(F32) + axis_swap(low, "ctx", 1).astype(F32)


def tp_half(whole):
    core = lax.axis_index("tp") % 2
    rows = whole.shape[0] // 2
    return (
        lax.dynamic_slice_in_dim(whole, core * rows, rows, 0),
        lax.dynamic_slice_in_dim(whole, (1 - core) * rows, rows, 0),
    )


def tp_sum_core(part):
    mine, other = tp_half(part)
    half = mine.astype(F32) + axis_swap(other, "tp", 1).astype(F32)
    return lax.optimization_barrier(half.astype(BF16))


def tp_sum_chips(low, after=()):
    own, _ = lax.optimization_barrier((low, after))
    half = own.astype(F32)
    bit = 2
    while bit < lax.axis_size("tp"):
        if bit > 2:
            low = lax.optimization_barrier(half.astype(BF16))
            half = low.astype(F32)
        half = half + axis_swap(low, "tp", bit).astype(F32)
        bit *= 2
    return half


def tp_join(half):
    half = lax.optimization_barrier(half)
    other = axis_swap(half, "tp", 1)
    core, rows = lax.axis_index("tp") % 2, half.shape[0]
    whole = jnp.zeros((2 * rows, half.shape[1]), half.dtype)
    whole = lax.dynamic_update_slice_in_dim(whole, half, core * rows, 0)
    return lax.dynamic_update_slice_in_dim(whole, other, (1 - core) * rows, 0)


def on_device(
    hidden_in,
    segments,
    positions,
    norm_gains,
    norm_biases,
    qkv_weight,
    qkv_bias,
    out_weight,
    up_weight,
    up_bias,
    down_weight,
    branch_biases,
    out_grad,
):
    rows, tokens, model = hidden_in.shape
    assert rows == 1
    fsdp = lax.axis_size("fsdp")
    ctx_size = lax.axis_size("ctx")
    tp = lax.axis_size("tp")
    ctx_index = lax.axis_index("ctx")
    heads, head_dim = qkv_bias.shape[1], qkv_bias.shape[2] * fsdp
    width = heads * head_dim
    hidden_units = up_weight.shape[1]
    shard_rows = qkv_weight.shape[1]
    barrier = lax.optimization_barrier

    segs = segments.reshape(tokens)
    shift = [(i, i + 1) for i in range(ctx_size - 1)]
    back = [(i + 1, i) for i in range(ctx_size - 1)]
    w_qkv = gather_rows(jnp.transpose(qkv_weight, (1, 0, 2)).reshape(shard_rows, 3 * width))
    norms = jnp.concatenate([norm_gains, norm_biases, branch_biases], axis=0)
    biases = jnp.concatenate([qkv_bias.reshape(3 * heads, -1), up_bias], axis=0)
    bias_rows, bias_cols = biases.shape
    pack = jnp.concatenate(
        [norms, jnp.pad(biases, ((0, 0), (0, shard_rows - bias_cols)))], axis=0
    )
    pack = gather_small(jnp.pad(pack, ((0, -pack.shape[0] % 16), (0, 0)))).astype(F32)
    norms = jnp.transpose(pack[:, :6], (1, 0, 2)).reshape(6, model)
    gains, branch_bias = norms[0:2], norms[4:6]
    biases = jnp.transpose(pack[:, 6 : 6 + bias_rows, :bias_cols], (1, 0, 2)).reshape(-1)
    b_qkv, b_up = biases[: 3 * width], biases[3 * width :]
    second = jnp.concatenate([up_weight, out_weight.T], axis=1)
    w_qkv, second, segs = barrier((w_qkv, second, segs))
    earlier_segs = lax.ppermute(segs, "ctx", shift)
    second = gather_rows(second)
    third, second = barrier((down_weight.T, second))
    w_up, w_out = second[:, :hidden_units], second[:, hidden_units:]

    earlier_segs = jnp.where(ctx_index == 0, -1, earlier_segs)
    segs_all = jnp.concatenate([earlier_segs, segs])
    start = jnp.sum((segs_all[:, None] < segs[None, :]).astype(jnp.int32), axis=0)
    bq, bk = block_sizes(tokens)
    blocks = tokens // bq
    start_block = start.reshape(blocks, bq)[:, 0]
    ends = (jnp.arange(blocks, dtype=jnp.int32) + 1) * bq
    own_hi = (ends + bk - 1) // bk
    fwd_lo, fwd_hi = start_block // bk, own_hi + tokens // bk
    own_lo = jnp.maximum(start_block - tokens, 0) // bk
    cross_hi = jnp.full((blocks,), tokens // bk, jnp.int32)
    cross_lo = jnp.minimum(start_block // bk, cross_hi)
    start_row = start.reshape(1, tokens)

    rot_width = head_dim // 4
    frequency = jnp.power(10000.0, -jnp.arange(0, rot_width, 2).astype(F32) / rot_width)
    angles = positions.reshape(1, tokens).astype(F32) * frequency[:, None]
    cosine, sine_wave = jnp.cos(angles), jnp.sin(angles)
    q, kv, normed_attn, normed_mlp, normal_unit = project(
        heads,
        head_dim,
        hidden_in.reshape(tokens, model),
        w_qkv,
        b_qkv[:, None],
        norms,
        cosine,
        sine_wave,
    )
    kv0 = lax.ppermute(kv, "ctx", shift)

    grad_low = out_grad.reshape(tokens, model)
    up_pre = jnp.dot(normed_mlp, w_up, preferred_element_type=F32) + b_up
    cdf = 0.5 * (1.0 + lax.erf(up_pre * math.sqrt(0.5)))
    activated = (up_pre * cdf).astype(BF16)
    slope = (cdf + up_pre * (jnp.exp(-0.5 * up_pre * up_pre) * (1 / math.sqrt(2 * math.pi)))).astype(
        BF16
    )
    do = jnp.einsum("nd,de->en", grad_low, w_out, preferred_element_type=F32).astype(BF16)
    activated, slope, do = barrier((activated, slope, do))
    down_part = jnp.einsum("nd,nf->df", grad_low, activated, preferred_element_type=F32)
    w_down = gather_rows(third)
    down_part, do, w_down = barrier((down_part.astype(BF16), do, w_down))
    mixed, lse, dot = attention_forward(
        heads, head_dim, fwd_lo, fwd_hi, start_row, q, kv0, kv, do
    )

    down_sum = scatter_rows(down_part, mixed)
    down_sum, lse = barrier((down_sum, lse))
    dq0, dkv0 = attention_backward(
        heads, head_dim, tokens, BF16, cross_lo, cross_hi, start_row, q, do, lse, dot, kv0
    )
    dkv_back = lax.ppermute(dkv0, "ctx", back)

    activated, slope, dq0 = barrier((activated, slope, dq0))
    branch_part = jnp.einsum("en,de->nd", mixed, w_out, preferred_element_type=F32) + jnp.einsum(
        "nf,df->nd", activated, w_down, preferred_element_type=F32
    )
    branch_part, slope = barrier((branch_part.astype(BF16), slope))
    act_grad = jnp.einsum("nd,df->nf", grad_low, w_down, preferred_element_type=F32)
    up_grad = barrier((act_grad * slope.astype(F32)).astype(BF16))
    up_part = jnp.einsum("nd,nf->df", normed_mlp, up_grad, preferred_element_type=F32)
    up_part = up_part.astype(BF16)
    branch_low = tp_sum_core(branch_part)
    mlp_norm_grad = jnp.einsum("nf,df->nd", up_grad, w_up, preferred_element_type=F32)
    up_bias_part = jnp.sum(up_grad, axis=0, dtype=F32)
    branch_row = jnp.sum(grad_low, axis=0, dtype=F32)
    out_part = jnp.einsum("nd,en->de", grad_low, mixed, preferred_element_type=F32).astype(BF16)
    up_part, branch_low, lse, dkv_back, mlp_norm_grad, out_part, up_bias_part, branch_row = barrier(
        (up_part, branch_low, lse, dkv_back, mlp_norm_grad, out_part, up_bias_part, branch_row)
    )
    dq1, dkv1 = attention_backward(
        heads, head_dim, 0, F32, own_lo, own_hi, start_row - tokens, q, do, lse, dot, kv
    )
    branch_half = tp_sum_chips(branch_low, dq1)
    up_sum = scatter_rows(up_part, dq1)
    up_sum, branch_half, dkv1, dq1 = barrier((up_sum, branch_half, dkv1, dq1))
    mlp_sum = jnp.concatenate([up_sum, down_sum], axis=1)
    residual_half, _ = tp_half(hidden_in.reshape(tokens, model))
    hidden_half = (
        residual_half.astype(F32) + branch_half + branch_bias[0] + branch_bias[1]
    ).astype(BF16)

    dkv = dkv1 + dkv_back.astype(F32)
    projected_grad = jnp.concatenate(
        [
            rotate(dq0 + dq1, cosine, sine_wave, -1.0, heads, head_dim),
            rotate(dkv[:width], cosine, sine_wave, -1.0, heads, head_dim),
            dkv[width:],
        ],
        axis=0,
    ).astype(BF16)
    projected_grad = barrier(projected_grad)

    attn_norm_grad = jnp.einsum("en,de->nd", projected_grad, w_qkv, preferred_element_type=F32)
    unit_part = attn_norm_grad * gains[0] + mlp_norm_grad * gains[1]
    unit_low = tp_sum_core(barrier(unit_part.astype(BF16)))
    qkv_part = jnp.einsum("nd,en->de", normed_attn, projected_grad, preferred_element_type=F32)
    qkv_bias_part = jnp.sum(projected_grad, axis=1, dtype=F32)

    norm_parts = jnp.stack(
        [
            jnp.sum(attn_norm_grad * normal_unit.astype(F32), axis=0),
            jnp.sum(mlp_norm_grad * normal_unit.astype(F32), axis=0),
            jnp.sum(attn_norm_grad, axis=0),
            jnp.sum(mlp_norm_grad, axis=0),
            branch_row,
        ],
        axis=1,
    )
    bias_parts = jnp.concatenate([qkv_bias_part, up_bias_part]).reshape(bias_rows, fsdp, bias_cols)
    bias_parts = jnp.transpose(bias_parts, (1, 0, 2)).reshape(fsdp, -1)
    bias_count = bias_parts.shape[1]
    bias_wide = -(-bias_count // shard_rows)
    bias_parts = jnp.pad(bias_parts, ((0, 0), (0, bias_wide * shard_rows - bias_count)))
    bias_parts = bias_parts.reshape(model, bias_wide)
    extra = jnp.concatenate([norm_parts, bias_parts], axis=1)
    extra = jnp.pad(extra, ((0, 0), (0, 128 - extra.shape[1])))
    last_part = jnp.concatenate(
        [qkv_part.astype(BF16), out_part, extra.astype(BF16)], axis=1
    )
    unit_low, last_part, mlp_sum, hidden_half, hidden_tail = barrier(
        (unit_low, last_part, mlp_sum, hidden_half, hidden_in.reshape(tokens, model))
    )
    unit_grad = tp_sum_chips(unit_low)
    mlp_grad = ctx_sum(mlp_sum)
    hidden_out = tp_join(hidden_half)
    last_sum = scatter_rows(last_part, (mlp_grad, hidden_out))
    hidden_tail, _ = tp_half(hidden_tail)
    residual_tail = hidden_tail.astype(F32)
    centred_tail = residual_tail - jnp.mean(residual_tail, axis=-1, keepdims=True)
    spread_tail = lax.rsqrt(jnp.mean(centred_tail * centred_tail, axis=-1, keepdims=True) + 1e-05)
    unit = centred_tail * spread_tail
    grad_tail, _ = tp_half(grad_low)
    input_half = grad_tail.astype(F32) + spread_tail * (
        unit_grad
        - jnp.mean(unit_grad, axis=-1, keepdims=True)
        - unit * jnp.mean(unit_grad * unit, axis=-1, keepdims=True)
    )
    input_grad = tp_join(input_half.astype(BF16))
    last_grad = ctx_sum(last_sum)
    qkv_weight_grad = jnp.transpose(
        last_grad[:, : 3 * width].reshape(shard_rows, 3, width), (1, 0, 2)
    )
    out_weight_grad = last_grad[:, 3 * width : 4 * width].T
    up_weight_grad = mlp_grad[:, :hidden_units]
    down_weight_grad = mlp_grad[:, hidden_units:].T
    extra = last_grad[:, 4 * width :]
    norm_sums = sum_pairs(extra[:, :4].T, "tp")
    branch_sum = extra[:, 4]
    bias_sums = extra[:, 5 : 5 + bias_wide].reshape(-1)[:bias_count].reshape(bias_rows, bias_cols)
    qkv_bias_grad = bias_sums[: 3 * heads].reshape(3, heads, bias_cols)
    up_bias_grad = bias_sums[3 * heads :]
    return (
        hidden_out.reshape(hidden_in.shape),
        input_grad.reshape(hidden_in.shape),
        norm_sums[0:2],
        norm_sums[2:4],
        qkv_weight_grad,
        qkv_bias_grad,
        out_weight_grad,
        up_weight_grad,
        up_bias_grad,
        down_weight_grad,
        jnp.stack([branch_sum, branch_sum]),
    )


def solution(mesh):
    return jax.shard_map(
        on_device,
        mesh=mesh,
        in_specs=(
            P("fsdp", "ctx", None),
            P("fsdp", "ctx"),
            P("fsdp", "ctx"),
            P(None, "fsdp"),
            P(None, "fsdp"),
            P(None, "fsdp", "tp"),
            P(None, "tp", "fsdp"),
            P("tp", "fsdp"),
            P("fsdp", "tp"),
            P("tp", "fsdp"),
            P("tp", "fsdp"),
            P(None, "fsdp"),
            P("fsdp", "ctx", None),
        ),
        out_specs=(
            P("fsdp", "ctx", None),
            P("fsdp", "ctx", None),
            P(None, "fsdp"),
            P(None, "fsdp"),
            P(None, "fsdp", "tp"),
            P(None, "tp", "fsdp"),
            P("tp", "fsdp"),
            P("fsdp", "tp"),
            P("tp", "fsdp"),
            P("tp", "fsdp"),
            P(None, "fsdp"),
        ),
        check_vma=False,
    )
```
